32 devices in a mesh: fsdp: 2 (over y), seq: 16 (over z, x, core).
Axes of the slice: x: 2, y: 2, z: 4, core: 2. Of those that a mesh axis runs over, the one named last changes fastest.
Arguments:
- inputs: bfloat16 [8, 1024, 1024], P('fsdp', 'seq'), may hold values from -6 to 6
- mixer_gain: bfloat16 [1024], P('fsdp'), may hold values from 0.5 to 1.5
- query_weight: bfloat16 [1024, 512], P('fsdp'), may hold values from -0.1875 to 0.1875
- key_weight: bfloat16 [1024, 512], P('fsdp'), may hold values from -0.1875 to 0.1875
- value_weight: bfloat16 [1024, 1024], P('fsdp'), may hold values from -0.1875 to 0.1875
- decay_down: bfloat16 [1024, 16], P('fsdp'), may hold values from -0.1875 to 0.1875
- decay_up: bfloat16 [16, 512], P('fsdp'), may hold values from -1.5 to 1.5
- decay_bias: bfloat16 [512], P('fsdp'), may hold values from -1 to 5
- outgate_weight: bfloat16 [1024, 1024], P('fsdp'), may hold values from -0.1875 to 0.1875
- head_gain: bfloat16 [256], P('fsdp'), may hold values from 0.5 to 1.5
- output_weight: bfloat16 [1024, 1024], P('fsdp'), may hold values from -0.1875 to 0.1875
- feed_gain: bfloat16 [1024], P('fsdp'), may hold values from 0.5 to 1.5
- feed_gate: bfloat16 [1024, 2816], P('fsdp'), may hold values from -0.1875 to 0.1875
- feed_up: bfloat16 [1024, 2816], P('fsdp'), may hold values from -0.1875 to 0.1875
- feed_down: bfloat16 [2816, 1024], P('fsdp'), may hold values from -0.109375 to 0.109375
- cotangent: bfloat16 [8, 1024, 1024], P('fsdp', 'seq'), may hold values from -6 to 6
Outputs:
- output: bfloat16 [8, 1024, 1024], P('fsdp', 'seq')
- input_grad: float32 [8, 1024, 1024], P('fsdp', 'seq')
- grad_mixer_gain: float32 [1024], P('fsdp')
- grad_query_weight: float32 [1024, 512], P('fsdp')
- grad_key_weight: float32 [1024, 512], P('fsdp')
- grad_value_weight: float32 [1024, 1024], P('fsdp')
- grad_decay_down: float32 [1024, 16], P('fsdp')
- grad_decay_up: float32 [16, 512], P('fsdp')
- grad_decay_bias: float32 [512], P('fsdp')
- grad_outgate_weight: float32 [1024, 1024], P('fsdp')
- grad_head_gain: float32 [256], P('fsdp')
- grad_output_weight: float32 [1024, 1024], P('fsdp')
- grad_feed_gain: float32 [1024], P('fsdp')
- grad_feed_gate: float32 [1024, 2816], P('fsdp')
- grad_feed_up: float32 [1024, 2816], P('fsdp')
- grad_feed_down: float32 [2816, 1024], P('fsdp')
The draws below stay inside these ranges and needn't reach their ends.
All inputs are finite; a program needn't handle non-finite values.
Results may differ from the reference program's by a relative error of at most 0.014.
Values may be sent and summed in bfloat16 or wider, within the bound.
No kernel may reach another device: no remote copies, remote signals or barrier semaphores. Data moves between devices by JAX's collectives and lax.ppermute only.
A program may use at most 320 MiB of HBM per device.

```python
import jax
import jax.numpy as jnp
from jax import lax

D = 1024
H = 4
DK = 128
DV = 256
RANK = 16
FF = 2816
SPAN = 64
LEN = 1024
SEQUENCES = 8


def level_of(key, extent, cuts, low, high):
    factor_of = 1.0
    for position, parts in cuts:
        steps = jax.random.uniform(jax.random.fold_in(jax.random.fold_in(key, 6), position), (parts,), jnp.float32, low / len(cuts), high / len(cuts))
        factor_of = factor_of * jnp.repeat(jnp.exp(steps), extent[position] // parts).reshape((-1,) + (1,) * (len(extent) - 1 - position))
    return factor_of


def gaussian(own_key, dims, scale, bound, cuts=(), held_as=jnp.bfloat16):
    array = jax.random.normal(own_key, dims, jnp.float32) * scale
    if len(cuts) > 0:
        array = level_of(own_key, dims, cuts, -0.22, 0.18) * array
    return jnp.clip(array, min=-bound, max=bound).astype(held_as)


def setup_inputs(seed: int = 0) -> dict:
    seeds = jax.random.split(jax.random.key(seed), 17)
    inputs = gaussian(seeds[0], (SEQUENCES, LEN, D), 1.0, 6.0, ((0, 2), (1, 16)))
    mixer_gain = jnp.clip(1.0 + 0.1 * jax.random.normal(seeds[1], (D,), jnp.float32), 0.5, 1.5).astype(jnp.bfloat16)
    query_weight = gaussian(seeds[2], (D, H * DK), D ** -0.5, 0.1875, ((0, 2),))
    key_weight = gaussian(seeds[3], (D, H * DK), D ** -0.5, 0.1875, ((0, 2),))
    value_weight = gaussian(seeds[4], (D, H * DV), D ** -0.5, 0.1875, ((0, 2),))
    decay_down = gaussian(seeds[5], (D, RANK), D ** -0.5, 0.1875, ((0, 2),))
    decay_up = gaussian(seeds[6], (RANK, H * DK), RANK ** -0.5, 1.5, ((0, 2),))
    decay_bias = jnp.clip(-1.0 + 6.0 * jax.random.uniform(seeds[7], (H * DK,), jnp.float32) ** level_of(seeds[7], (H * DK,), ((0, 2),), -0.2, 0.2), -1.0, 5.0).astype(jnp.bfloat16)
    outgate_weight = gaussian(seeds[8], (D, H * DV), D ** -0.5, 0.1875, ((0, 2),))
    head_gain = jnp.clip(1.0 + 0.1 * jax.random.normal(seeds[9], (DV,), jnp.float32), 0.5, 1.5).astype(jnp.bfloat16)
    output_weight = gaussian(seeds[10], (H * DV, D), (H * DV) ** -0.5, 0.1875, ((0, 2),))
    feed_gain = jnp.clip(1.0 + 0.1 * jax.random.normal(seeds[11], (D,), jnp.float32), 0.5, 1.5).astype(jnp.bfloat16)
    feed_gate = gaussian(seeds[12], (D, FF), D ** -0.5, 0.1875, ((0, 2),))
    feed_up = gaussian(seeds[13], (D, FF), D ** -0.5, 0.1875, ((0, 2),))
    feed_down = gaussian(seeds[14], (FF, D), FF ** -0.5, 0.109375, ((0, 2),))
    cotangent = gaussian(seeds[15], (SEQUENCES, LEN, D), 1.0, 6.0, ((0, 2), (1, 16)))
    return {"inputs": inputs, "mixer_gain": mixer_gain, "query_weight": query_weight, "key_weight": key_weight, "value_weight": value_weight, "decay_down": decay_down, "decay_up": decay_up, "decay_bias": decay_bias, "outgate_weight": outgate_weight, "head_gain": head_gain, "output_weight": output_weight, "feed_gain": feed_gain, "feed_gate": feed_gate, "feed_up": feed_up, "feed_down": feed_down, "cotangent": cotangent}


epsilon = 1e-06
head_floor = 0.25
gate_scale = 16.0
highest = lax.Precision.HIGHEST

@jax.custom_vjp
def low(v):
    return lax.optimization_barrier(v.astype(jnp.bfloat16)).astype(jnp.float32)

@jax.custom_vjp
def low_back(v):
    return v

def low_keep(v):
    return (low(v), None)

def low_pass(kept, grad):
    return (grad,)

def back_keep(v):
    return (v, None)

def back_low(kept, grad):
    return (low(grad),)
low.defvjp(low_keep, low_pass)
low_back.defvjp(back_keep, back_low)

def product(left, right):
    return jnp.dot(left, right, precision=highest)

def rms_scale(values, scale_gain):
    return values * lax.rsqrt(lax.optimization_barrier(jnp.mean(values * values, axis=-1, keepdims=True)) + epsilon) * scale_gain

def head_scale(values, scale_gain):
    return values * lax.rsqrt(jnp.maximum(lax.optimization_barrier(jnp.mean(values * values, axis=-1, keepdims=True)), head_floor)) * scale_gain

def swiglu(gate_part, up_part):
    return jax.nn.silu(gate_part) * up_part

def head_mix(mixed, out_gate, head_gain):
    row_count = mixed.shape[0]
    normed = head_scale(mixed, head_gain)
    return (normed * jax.nn.silu(out_gate.reshape(mixed.shape))).reshape(row_count, -1)

def span_mix(query, keys, decay, values):
    length, key_width = query.shape
    blocks = length // SPAN
    shaped_q = query.reshape(blocks, SPAN, key_width) * key_width ** (-0.5)
    shaped_k = keys.reshape(blocks, SPAN, key_width)
    shaped_v = values.reshape(blocks, SPAN, values.shape[1])
    cumulative = jnp.cumsum(decay.reshape(blocks, SPAN, key_width), axis=1)
    span_end = cumulative[:, SPAN - 1:, :]
    q_tilde = shaped_q * jnp.exp(cumulative)
    k_tilde = shaped_k * jnp.exp(-cumulative)
    k_tail = shaped_k * jnp.exp(span_end - cumulative)
    scores = jnp.einsum('bik,bjk->bij', q_tilde, k_tilde, precision=highest)
    row_index = lax.broadcasted_iota(jnp.int32, (SPAN, SPAN), 0)
    col_index = lax.broadcasted_iota(jnp.int32, (SPAN, SPAN), 1)
    scores = jnp.where(row_index >= col_index, scores, 0.0)
    inside = jnp.einsum('bij,bjv->biv', scores, shaped_v, precision=highest)
    updates = jnp.einsum('bjk,bjv->bkv', k_tail, shaped_v, precision=highest)
    span_fade = jnp.exp(span_end[:, 0, :])

    def advance(carried, pieces):
        fade_rate, update = pieces
        return (carried * fade_rate[:, None] + update, carried)
    initial = jnp.zeros((key_width, values.shape[1]), jnp.float32)
    _, before = lax.scan(advance, initial, (span_fade, updates))
    outside = jnp.einsum('bik,bkv->biv', q_tilde, before, precision=highest)
    return (inside + outside).reshape(length, values.shape[1])

def layer(sequence, params):
    mixer_gain, query_weight, key_weight, value_weight, decay_down, decay_up, decay_bias, outgate_weight, head_gain, output_weight, feed_gain, feed_gate, feed_up, feed_down = params
    length = sequence.shape[0]
    normed = low(rms_scale(sequence, mixer_gain))
    query = low_back(low(product(normed, query_weight)))
    keys = low_back(low(product(normed, key_weight)))
    values = low_back(low(product(normed, value_weight)))
    ranked = low_back(low(product(normed, decay_down)))
    decay = low_back(low(jax.nn.log_sigmoid(product(ranked, decay_up) + decay_bias) / gate_scale))
    out_gate = low_back(product(normed, outgate_weight))
    mixing = jax.vmap(span_mix, in_axes=1, out_axes=1)
    mixed = mixing(query.reshape(length, H, DK), keys.reshape(length, H, DK), decay.reshape(length, H, DK), values.reshape(length, H, DV))
    mixed = low_back(low(mixed))
    gated = low(head_mix(mixed, out_gate, head_gain))
    middle = sequence + low_back(product(gated, output_weight))
    second_norm = low(rms_scale(middle, feed_gain))
    gate_part = low_back(product(second_norm, feed_gate))
    up_part = low_back(product(second_norm, feed_up))
    hidden = low(swiglu(gate_part, up_part))
    return middle + low_back(product(hidden, feed_down))

def reference(inputs, mixer_gain, query_weight, key_weight, value_weight, decay_down, decay_up, decay_bias, outgate_weight, head_gain, output_weight, feed_gain, feed_gate, feed_up, feed_down, cotangent):
    params = tuple((weight.astype(jnp.float32) for weight in (mixer_gain, query_weight, key_weight, value_weight, decay_down, decay_up, decay_bias, outgate_weight, head_gain, output_weight, feed_gain, feed_gate, feed_up, feed_down)))

    def one_sequence(totals, operands):
        sequence, seq_grad = operands
        result, pullback = jax.vjp(layer, sequence.astype(jnp.float32), params)
        d_input, d_params = pullback(seq_grad.astype(jnp.float32))
        return (jax.tree.map(jnp.add, totals, d_params), (result.astype(jnp.bfloat16), d_input))
    initial = tuple((jnp.zeros_like(weight) for weight in params))
    totals, (output, input_grad) = lax.scan(one_sequence, initial, (inputs, cotangent))
    grad_mixer_gain, grad_query_weight, grad_key_weight, grad_value_weight, grad_decay_down, grad_decay_up, grad_decay_bias, grad_outgate_weight, grad_head_gain, grad_output_weight, grad_feed_gain, grad_feed_gate, grad_feed_up, grad_feed_down = totals
    return (output, input_grad, grad_mixer_gain, grad_query_weight, grad_key_weight, grad_value_weight, grad_decay_down, grad_decay_up, grad_decay_bias, grad_outgate_weight, grad_head_gain, grad_output_weight, grad_feed_gain, grad_feed_gate, grad_feed_up, grad_feed_down)
```

```python
import functools

import jax
import jax.numpy as jnp
from jax import lax
from jax.experimental import pallas as pl
from jax.experimental.pallas import tpu as pltpu
from jax.sharding import PartitionSpec as P

H = 4
DK = 128
DV = 256
SPAN = 64


epsilon = 1e-06
head_floor = 0.25
gate_scale = 16.0
highest = lax.Precision.HIGHEST
bf16 = jnp.bfloat16
f32 = jnp.float32


def rms_scale(values, scale_gain):
    return (
        values * lax.rsqrt(jnp.mean(values * values, axis=-1, keepdims=True) + epsilon) * scale_gain
    )


def head_scale(values, scale_gain):
    return (
        values
        * lax.rsqrt(jnp.maximum(jnp.mean(values * values, axis=-1, keepdims=True), head_floor))
        * scale_gain
    )


def swiglu(gate_part, up_part):
    return jax.nn.silu(gate_part) * up_part


def head_mix(mixed, out_gate, head_gain):
    row_count = mixed.shape[0]
    normed = head_scale(mixed, head_gain)
    return (normed * jax.nn.silu(out_gate.reshape(mixed.shape))).reshape(row_count, -1)


def mat_product(left, right):
    return jnp.dot(left, right, preferred_element_type=f32)


def cross_rows(left, right):
    return lax.dot_general(left, right, (((0,), (0,)), ((), ())), preferred_element_type=f32)


def back_product(left, right):
    return lax.dot_general(left, right, (((1,), (1,)), ((), ())), preferred_element_type=f32)


def fine(left, right, contract):
    return lax.dot_general(
        left, right, (((contract[0],), (contract[1],)), ((), ())),
        precision=highest, preferred_element_type=f32,
    )


def triangle():
    rows = lax.broadcasted_iota(jnp.int32, (SPAN, SPAN), 0)
    cols = lax.broadcasted_iota(jnp.int32, (SPAN, SPAN), 1)
    return rows >= cols


def block_terms(q_ref, k_ref, g_ref, head):
    cols = slice(head * DK, (head + 1) * DK)
    lower = jnp.where(triangle(), 1.0, 0.0).astype(bf16)
    c = jnp.dot(lower, g_ref[:, cols], preferred_element_type=f32)
    e = c[SPAN - 1 : SPAN, :]
    qt = q_ref[:, cols].astype(f32) * DK ** (-0.5) * jnp.exp(c)
    keys = k_ref[:, cols].astype(f32)
    return c, e, qt, keys * jnp.exp(-c), keys * jnp.exp(e - c)


def local_kernel(q_ref, k_ref, g_ref, v_ref, inside_ref, update_ref, fade_ref):
    for head in range(H):
        wide = slice(head * DV, (head + 1) * DV)
        c, e, qt, kt, kl = block_terms(q_ref, k_ref, g_ref, head)
        v = v_ref[:, wide].astype(f32)
        scores = jnp.where(triangle(), fine(qt, kt, (1, 1)), 0.0)
        inside_ref[:, wide] = fine(scores, v, (1, 0))
        update_ref[head] = fine(kl, v, (0, 0)).astype(bf16)
        fade_ref[0, head : head + 1, :] = jnp.exp(e)


def outside_kernel(q_ref, k_ref, g_ref, inside_ref, state_ref, mixed_ref):
    for head in range(H):
        wide = slice(head * DV, (head + 1) * DV)
        c, e, qt, kt, kl = block_terms(q_ref, k_ref, g_ref, head)
        state = state_ref[head].astype(f32)
        mixed_ref[:, wide] = (inside_ref[:, wide] + fine(qt, state, (1, 0))).astype(bf16)


def back_state_kernel(q_ref, k_ref, g_ref, do_ref, update_ref):
    for head in range(H):
        wide = slice(head * DV, (head + 1) * DV)
        c, e, qt, kt, kl = block_terms(q_ref, k_ref, g_ref, head)
        update_ref[head] = fine(qt, do_ref[:, wide].astype(f32), (0, 0)).astype(bf16)


def back_kernel(
    q_ref, k_ref, g_ref, v_ref, do_ref, state_ref, after_ref, dq_ref, dk_ref, dg_ref, dv_ref
):
    mask = triangle()
    upper = jnp.where(
        lax.broadcasted_iota(jnp.int32, (SPAN, SPAN), 0)
        <= lax.broadcasted_iota(jnp.int32, (SPAN, SPAN), 1),
        1.0,
        0.0,
    )
    last = lax.broadcasted_iota(jnp.int32, (SPAN, DK), 0) == SPAN - 1
    for head in range(H):
        wide = slice(head * DV, (head + 1) * DV)
        cols = slice(head * DK, (head + 1) * DK)
        c, e, qt, kt, kl = block_terms(q_ref, k_ref, g_ref, head)
        v = v_ref[:, wide].astype(f32)
        do = do_ref[:, wide].astype(f32)
        state = state_ref[head].astype(f32)
        after = after_ref[head].astype(f32)
        scores = jnp.where(mask, fine(qt, kt, (1, 1)), 0.0)
        d_scores = jnp.where(mask, fine(do, v, (1, 1)), 0.0)
        dv_ref[:, wide] = (fine(scores, do, (0, 0)) + fine(kl, after, (1, 0))).astype(bf16)
        dqt = fine(d_scores, kt, (1, 0)) + fine(do, state, (1, 1))
        dkt = fine(d_scores, qt, (0, 0))
        dkl = fine(v, after, (1, 1))
        dq_ref[:, cols] = (dqt * (DK ** (-0.5) * jnp.exp(c))).astype(bf16)
        dk_ref[:, cols] = (dkt * jnp.exp(-c) + dkl * jnp.exp(e - c)).astype(bf16)
        tail = kl * dkl
        ones = jnp.ones((8, DV), f32)
        fade_grad = fine(ones, after * state, (1, 1))[0:1, :]
        de = jnp.sum(tail, axis=0, keepdims=True) + jnp.exp(e) * fade_grad
        dc = qt * dqt - kt * dkt - tail + jnp.where(last, de, 0.0)
        dg_ref[:, cols] = fine(upper, dc, (1, 0)).astype(bf16)


def row_spec(width):
    return pl.BlockSpec((SPAN, width), lambda i: (i, 0))


def head_spec():
    return pl.BlockSpec((H, DK, DV), lambda i: (i, 0, 0))


def block_call(kernel, seq_count, in_specs, out_specs, out_shape, flops):
    return pl.pallas_call(
        kernel,
        grid=(seq_count,),
        in_specs=in_specs,
        out_specs=out_specs,
        out_shape=out_shape,
        compiler_params=pltpu.CompilerParams(vmem_limit_bytes=24 * 1024 * 1024),
        cost_estimate=pl.CostEstimate(
            flops=flops * seq_count * H, bytes_accessed=4 * 1024 * 1024, transcendentals=0
        ),
    )


class Links:
    def __init__(self):
        self.fsdp = lax.axis_index("fsdp")
        self.seq = lax.axis_index("seq")
        self.seq_count = lax.axis_size("seq")
        self.bits = self.seq_count.bit_length() - 1

    def own(self, axis):
        return self.fsdp if axis == "fsdp" else lax.rem(lax.div(self.seq, 1 << axis), 2)

    def swap(self, array, axis):
        if axis == "fsdp":
            return lax.ppermute(array, "fsdp", [(0, 1), (1, 0)])
        return lax.ppermute(
            array, "seq", [(i, i ^ (1 << axis)) for i in range(self.seq_count)]
        )

    def shift(self, array, steps):
        moves = [
            (i, i + steps) for i in range(self.seq_count) if 0 <= i + steps < self.seq_count
        ]
        return lax.ppermute(array, "seq", moves)


def pick(array, index, axis=0):
    return lax.dynamic_index_in_dim(array, index, axis, keepdims=False)


def in_order(bit, own, other, axis):
    size = own.shape[axis]
    shape = list(own.shape)
    shape[axis] = 2 * size
    whole = jnp.zeros(shape, own.dtype)
    whole = lax.dynamic_update_slice_in_dim(whole, own, bit * size, axis)
    return lax.dynamic_update_slice_in_dim(whole, other, (1 - bit) * size, axis)


def gather_weight(links, mine, bits):
    rows = mine.shape[0] >> len(bits)
    place = sum(links.own(bit) << i for i, bit in enumerate(bits))
    piece = lax.dynamic_slice_in_dim(mine, place * rows, rows, 0)
    held = [(0, links.swap(piece, "fsdp"))]
    for i, bit in enumerate(bits):
        held = held + [(rel ^ (1 << i), links.swap(x, bit)) for rel, x in held]
    whole = jnp.zeros((2 * mine.shape[0],) + mine.shape[1:], mine.dtype)
    whole = lax.dynamic_update_slice_in_dim(whole, mine, links.fsdp * mine.shape[0], 0)
    base = (1 - links.fsdp) * mine.shape[0]
    for rel, x in held:
        whole = lax.dynamic_update_slice_in_dim(
            whole, x, base + jnp.bitwise_xor(place, rel) * rows, 0
        )
    return whole


def prefix_states(links, update, fade, backward):
    heads = update.shape[0]

    def position(bit):
        return 1 - links.own(bit) if backward else links.own(bit)

    def meet(bit, t, f):
        count = t.shape[0] // 2
        mine = links.own(bit)
        t2 = t.reshape((2, count) + t.shape[1:])
        other_t = links.swap(pick(t2, 1 - mine).astype(bf16), bit).astype(f32)
        other_f = links.swap(f, bit)
        f2 = f.reshape((2, count) + f.shape[1:])
        of2 = other_f.reshape(f2.shape)
        own_t, own_f = pick(t2, mine).astype(f32), pick(f2, mine)
        other_f = pick(of2, mine)
        second = position(bit) == 1
        first_t = jnp.where(second, other_t, own_t)
        first_f = jnp.where(second, other_f, own_f)
        last_t = jnp.where(second, own_t, other_t)
        last_f = jnp.where(second, own_f, other_f)
        return first_t, first_f, first_t * last_f[..., None] + last_t, first_f * last_f

    t0, f0, t, f = meet(0, update, fade)
    t1, f1, t, f = meet(1, t, f)
    sign = -1 if backward else 1
    t = links.shift(t.astype(bf16), 4 * sign).astype(f32)
    f = links.shift(f, 4 * sign)
    reach = 1
    groups = links.seq_count // 4
    while reach < groups - 1:
        got_t = links.shift(t.astype(bf16), 4 * reach * sign).astype(f32)
        got_f = links.shift(f, 4 * reach * sign)
        t = t + f[..., None] * got_t
        f = f * got_f
        reach *= 2

    def part(bit, before, first_t, first_f):
        later = before * first_f[..., None] + first_t
        second = position(bit) == 1
        mine = jnp.where(second, later, before).astype(bf16)
        other = links.swap(jnp.where(second, before, later).astype(bf16), bit)
        return in_order(links.own(bit), mine, other, 0)

    t = part(1, t, t1, f1)
    return part(0, t.astype(f32), t0, f0)


def sum_rows(links, partial, order):
    rows, cols = partial.shape
    axes = ["fsdp"] + list(range(1, links.bits))
    shares = 1 << len(axes)
    data = partial.reshape([2] * len(axes) + [rows // shares, cols])
    left = list(axes)
    for axis in order:
        dim = left.index(axis)
        mine = links.own(axis)
        got = links.swap(pick(data, 1 - mine, dim), axis)
        data = (pick(data, mine, dim).astype(f32) + got.astype(f32)).astype(bf16)
        left.remove(axis)
    data = data.reshape((rows // shares, cols))
    return data


def share_rows(links, data):
    for axis in range(links.bits - 1, 0, -1):
        data = in_order(links.own(axis), data, links.swap(data, axis), 0)
    return data


def columns_of_cores(links, data):
    other = links.swap(data, 0)
    first = links.own(0) == 0
    return jnp.where(first, data, other).astype(f32), jnp.where(first, other, data).astype(f32)


def half_columns(links, array, parts):
    mine = links.own(0)
    ours, theirs = [], []
    offset = 0
    for width in parts:
        piece = array[:, offset : offset + width]
        ours.append(lax.dynamic_slice_in_dim(piece, mine * (width // 2), width // 2, 1))
        theirs.append(lax.dynamic_slice_in_dim(piece, (1 - mine) * (width // 2), width // 2, 1))
        offset += width
    return jnp.concatenate(ours, axis=1), jnp.concatenate(theirs, axis=1)


def both_cores(links, array):
    return jnp.concatenate((array, links.swap(array, 0)), axis=0)


def wide_grad(links, left_both, right, parts):
    ours, theirs = half_columns(links, right, parts)
    right_both = jnp.concatenate((ours, links.swap(theirs, 0)), axis=0)
    return cross_rows(left_both, right_both).astype(bf16)


def per_device(
    inputs,
    mixer_gain,
    query_weight,
    key_weight,
    value_weight,
    decay_down,
    decay_up,
    decay_bias,
    outgate_weight,
    head_gain,
    output_weight,
    feed_gain,
    feed_gate,
    feed_up,
    feed_down,
    cotangent,
):
    links = Links()
    seq_count, seg_rows, width = inputs.shape
    row_count = seq_count * seg_rows
    rank = decay_down.shape[1]
    hidden_width = feed_gate.shape[1]
    key_cols, value_cols = H * DK, H * DV

    small = (mixer_gain, decay_down, decay_up, decay_bias, head_gain, feed_gain)
    packed = jnp.concatenate([piece.reshape(-1) for piece in small])
    packed_other = links.swap(packed, "fsdp")
    low_half = jnp.where(links.fsdp == 0, packed, packed_other)
    high_half = jnp.where(links.fsdp == 0, packed_other, packed)
    whole_small = []
    offset = 0
    for piece in small:
        parts = [half[offset : offset + piece.size].reshape(piece.shape) for half in (low_half, high_half)]
        whole_small.append(jnp.concatenate(parts, axis=0))
        offset += piece.size
    full_mixer_gain, full_down, full_up_rank, full_bias, full_head_gain, full_feed_gain = whole_small

    in_widths = (key_cols, key_cols, value_cols, value_cols)
    near = [1, 0]
    far = [1, 2, 0]
    full_in = gather_weight(
        links,
        jnp.concatenate((query_weight, key_weight, value_weight, outgate_weight), axis=1),
        near,
    )
    full_output = gather_weight(links, output_weight, near)
    full_feed_gate = gather_weight(links, feed_gate, far)
    full_feed_up = gather_weight(links, feed_up, far)
    full_feed_down = gather_weight(links, feed_down, far)

    residual_in = inputs.reshape(row_count, width).astype(f32)
    normed_full, first_pull = jax.vjp(rms_scale, residual_in, full_mixer_gain.astype(f32))
    normed = normed_full.astype(bf16)
    projected = mat_product(normed, full_in)
    query = projected[:, :key_cols].astype(bf16)
    keys = projected[:, key_cols : 2 * key_cols].astype(bf16)
    values = projected[:, 2 * key_cols : 2 * key_cols + value_cols].astype(bf16)
    out_gate = projected[:, 2 * key_cols + value_cols :]
    ranked = mat_product(normed, full_down).astype(bf16)
    decay_in = mat_product(ranked, full_up_rank) + full_bias.astype(f32)
    decay = (jax.nn.log_sigmoid(decay_in) / gate_scale).astype(bf16)

    qkg_specs = [row_spec(key_cols)] * 3
    state_shape = jax.ShapeDtypeStruct((seq_count * H, DK, DV), bf16)
    block_flops = 2 * SPAN * DK * DV * 6
    inside, update, fade = block_call(
        local_kernel,
        seq_count,
        qkg_specs + [row_spec(value_cols)],
        [row_spec(value_cols), head_spec(), pl.BlockSpec((1, H, DK), lambda i: (i, 0, 0))],
        [
            jax.ShapeDtypeStruct((row_count, value_cols), f32),
            state_shape,
            jax.ShapeDtypeStruct((seq_count, H, DK), f32),
        ],
        2 * block_flops,
    )(query, keys, decay, values)
    fade = fade.reshape(seq_count * H, DK)
    state = prefix_states(links, update, fade, False)
    mixed = block_call(
        outside_kernel,
        seq_count,
        qkg_specs + [row_spec(value_cols), head_spec()],
        row_spec(value_cols),
        jax.ShapeDtypeStruct((row_count, value_cols), bf16),
        block_flops,
    )(query, keys, decay, inside, state)
    mixed_rows = mixed.reshape(row_count, H, DV).astype(f32)
    gated_full, head_pull = jax.vjp(head_mix, mixed_rows, out_gate, full_head_gain.astype(f32))
    gated = gated_full.astype(bf16)
    middle = residual_in + mat_product(gated, full_output)
    second_full, second_pull = jax.vjp(rms_scale, middle, full_feed_gain.astype(f32))
    second_norm = second_full.astype(bf16)
    gate_part = mat_product(second_norm, full_feed_gate)
    up_part = mat_product(second_norm, full_feed_up)
    hidden_full, act_pull = jax.vjp(swiglu, gate_part, up_part)
    hidden = hidden_full.astype(bf16)
    final = middle + mat_product(hidden, full_feed_down)
    output = final.astype(bf16).reshape(seq_count, seg_rows, width)

    d_down = cotangent.reshape(row_count, width)
    seq_grad = d_down.astype(f32)
    d_hidden = back_product(d_down, full_feed_down)
    d_gate_full, d_up_full = act_pull(d_hidden)
    d_gate = d_gate_full.astype(bf16)
    d_up = d_up_full.astype(bf16)
    d_second = back_product(d_gate, full_feed_gate) + back_product(d_up, full_feed_up)
    d_middle_norm, grad_feed_gain = second_pull(d_second)
    d_middle = seq_grad + d_middle_norm
    d_branch = d_middle.astype(bf16)
    d_gated = back_product(d_branch, full_output)
    d_mixed, d_outgate_full, grad_head_gain = head_pull(d_gated)
    d_mixed_low = d_mixed.astype(bf16).reshape(row_count, value_cols)
    d_outgate = d_outgate_full.astype(bf16)

    yxz = ["fsdp"] + list(range(1, links.bits))
    normed_both = both_cores(links, normed)
    second_both = both_cores(links, second_norm)
    hidden_both = both_cores(links, hidden)
    gated_both = both_cores(links, gated)
    sum_down = sum_rows(links, wide_grad(links, hidden_both, d_down, (width,)), yxz)
    sum_gate = sum_rows(links, wide_grad(links, second_both, d_gate, (hidden_width,)), yxz)
    sum_up = sum_rows(links, wide_grad(links, second_both, d_up, (hidden_width,)), yxz)
    sum_output = sum_rows(links, wide_grad(links, gated_both, d_branch, (width,)), yxz)
    sum_outgate = sum_rows(links, wide_grad(links, normed_both, d_outgate, (value_cols,)), yxz)

    back_update = block_call(
        back_state_kernel,
        seq_count,
        qkg_specs + [row_spec(value_cols)],
        head_spec(),
        state_shape,
        block_flops,
    )(query, keys, decay, d_mixed_low)
    after = prefix_states(links, back_update, fade, True)
    d_query, d_keys, d_decay, d_values = block_call(
        back_kernel,
        seq_count,
        qkg_specs + [row_spec(value_cols)] * 2 + [head_spec()] * 2,
        [row_spec(key_cols)] * 3 + [row_spec(value_cols)],
        [jax.ShapeDtypeStruct((row_count, key_cols), bf16)] * 3
        + [jax.ShapeDtypeStruct((row_count, value_cols), bf16)],
        4 * block_flops,
    )(query, keys, decay, values, d_mixed_low, state, after)

    d_decay_in = d_decay.astype(f32) * jax.nn.sigmoid(-decay_in) / gate_scale
    grad_decay_bias = jnp.sum(d_decay_in, axis=0)
    grad_decay_up = lax.dot_general(
        ranked.astype(f32), d_decay_in, (((0,), (0,)), ((), ())), precision=highest
    )
    d_ranked = lax.dot_general(
        d_decay_in, full_up_rank.astype(f32), (((1,), (1,)), ((), ())), precision=highest
    ).astype(bf16)
    d_qkv = jnp.concatenate((d_query, d_keys, d_values), axis=1)
    sum_qkv = sum_rows(links, wide_grad(links, normed_both, d_qkv, in_widths[:3]), yxz)
    grad_decay_down = cross_rows(normed, d_ranked)
    d_normed = back_product(
        jnp.concatenate((d_qkv, d_outgate), axis=1), full_in
    ) + back_product(d_ranked, full_down)
    d_input_norm, grad_mixer_gain = first_pull(d_normed)
    input_grad = (d_middle + d_input_norm).reshape(seq_count, seg_rows, width)

    small_grads = (
        grad_mixer_gain, grad_decay_down, grad_decay_up, grad_decay_bias, grad_head_gain,
        grad_feed_gain,
    )
    total = jnp.concatenate([grad.reshape(2, -1) for grad in small_grads], axis=1)
    total = pick(total, links.fsdp) + links.swap(pick(total, 1 - links.fsdp), "fsdp")
    for bit in range(links.bits):
        total = total + links.swap(total, bit)
    small_out = []
    offset = 0
    for grad in small_grads:
        size = grad.size // 2
        small_out.append(
            total[offset : offset + size].reshape((grad.shape[0] // 2,) + grad.shape[1:])
        )
        offset += size
    out_mixer_gain, out_decay_down, out_decay_up, out_bias, out_head_gain, out_feed_gain = small_out

    def finish(shares, parts):
        low, high = columns_of_cores(links, share_rows(links, shares))
        offset = 0
        outs = []
        for part in parts:
            half = part // 2
            outs.append(
                jnp.concatenate(
                    (low[:, offset : offset + half], high[:, offset : offset + half]), axis=1
                )
            )
            offset += half
        return outs

    (out_down,) = finish(sum_down, (width,))
    (out_gate_w,) = finish(sum_gate, (hidden_width,))
    (out_up_w,) = finish(sum_up, (hidden_width,))
    (out_output,) = finish(sum_output, (width,))
    (out_outgate,) = finish(sum_outgate, (value_cols,))
    out_query, out_key, out_value = finish(sum_qkv, in_widths[:3])
    return (
        output,
        input_grad,
        out_mixer_gain,
        out_query,
        out_key,
        out_value,
        out_decay_down,
        out_decay_up,
        out_bias,
        out_outgate,
        out_head_gain,
        out_output,
        out_feed_gain,
        out_gate_w,
        out_up_w,
        out_down,
    )


def solution(mesh):
    rows = P("fsdp", None)
    gains = P("fsdp")
    tokens = P("fsdp", "seq", None)
    weights = (gains, rows, rows, rows, rows, rows, gains, rows, gains, rows, gains, rows, rows, rows)
    return jax.shard_map(
        per_device,
        mesh=mesh,
        in_specs=(tokens,) + weights + (tokens,),
        out_specs=(tokens, tokens) + weights,
        check_vma=False,
    )
```

```python
import functools

import jax
import jax.numpy as jnp
from jax import lax
from jax.experimental import pallas as pl
from jax.experimental.pallas import tpu as pltpu
from jax.sharding import PartitionSpec as P

H = 4
DK = 128
DV = 256
SPAN = 64


epsilon = 1e-06
head_floor = 0.25
gate_scale = 16.0
highest = lax.Precision.HIGHEST
bf16 = jnp.bfloat16
f32 = jnp.float32


def rms_scale(values, scale_gain):
    return (
        values * lax.rsqrt(jnp.mean(values * values, axis=-1, keepdims=True) + epsilon) * scale_gain
    )


def mat_product(left, right):
    return jnp.dot(left, right, preferred_element_type=f32)


def cross_rows(left, right):
    return lax.dot_general(left, right, (((0,), (0,)), ((), ())), preferred_element_type=f32)


def back_product(left, right):
    return lax.dot_general(left, right, (((1,), (1,)), ((), ())), preferred_element_type=f32)


def dot(left, right, contract):
    return lax.dot_general(
        left, right, (((contract[0],), (contract[1],)), ((), ())), preferred_element_type=f32
    )


def fine(left, right, contract):
    lefts, rights = parts_of(left), parts_of(right)
    total = dot(lefts[0], rights[0], contract)
    if len(lefts) > 1:
        total = total + dot(lefts[1], rights[0], contract)
    if len(rights) > 1:
        total = total + dot(lefts[0], rights[1], contract)
    return total


def parts_of(array):
    if array.dtype == bf16:
        return (array,)
    high = array.astype(bf16)
    return high, (array - high.astype(f32)).astype(bf16)


def triangle():
    rows = lax.broadcasted_iota(jnp.int32, (SPAN, SPAN), 0)
    cols = lax.broadcasted_iota(jnp.int32, (SPAN, SPAN), 1)
    return rows >= cols


def block_terms(q_ref, k_ref, g_ref, head):
    cols = slice(head * DK, (head + 1) * DK)
    lower = jnp.where(triangle(), 1.0, 0.0).astype(bf16)
    c = jnp.dot(lower, g_ref[:, cols], preferred_element_type=f32)
    e = c[SPAN - 1 : SPAN, :]
    qt = q_ref[:, cols].astype(f32) * DK ** (-0.5) * jnp.exp(c)
    keys = k_ref[:, cols].astype(f32)
    return c, e, qt, keys * jnp.exp(-c), keys * jnp.exp(e - c)


def store_groups(ref, head, state):
    groups, size = ref.shape[1], ref.shape[2]
    count = state.shape[0] // groups
    for group in range(groups):
        ref[head, group, 0:count, :] = state[group * count : (group + 1) * count, :].astype(bf16)


def local_kernel(q_ref, k_ref, g_ref, v_ref, inside_ref, send_ref):
    groups = send_ref.shape[1]
    count = DV // groups
    place = lax.broadcasted_iota(jnp.int32, (16, DK), 0)
    for head in range(H):
        wide = slice(head * DV, (head + 1) * DV)
        c, e, qt, kt, kl = block_terms(q_ref, k_ref, g_ref, head)
        v = v_ref[:, wide]
        scores = jnp.where(triangle(), fine(qt, kt, (1, 1)), 0.0)
        inside_ref[:, wide] = fine(scores, v, (1, 0))
        store_groups(send_ref, head, fine(v, kl, (0, 0)))
        fade = jnp.exp(e)
        high = fade.astype(bf16).astype(f32)
        tail = jnp.where(place == 0, high, jnp.where(place == 1, fade - high, 0.0)).astype(bf16)
        for group in range(groups):
            send_ref[head, group, count : count + 16, :] = tail


def scan_kernel(backward, fade_ref, update_ref, before_ref):
    blocks, count, _ = before_ref.shape

    def step(i, state):
        block = blocks - 1 - i if backward else i
        before_ref[block] = state.astype(bf16)
        tail = fade_ref[block, count : count + 16, :].astype(f32)
        fade = tail[0:1, :] + tail[1:2, :]
        return state * fade + update_ref[block, 0:count, :].astype(f32)

    lax.fori_loop(0, blocks, step, jnp.zeros((count, DK), f32), unroll=4)


def scan_blocks(backward, received_fade, received):
    blocks, rows, _ = received_fade.shape
    return pl.pallas_call(
        functools.partial(scan_kernel, backward),
        out_shape=jax.ShapeDtypeStruct((blocks, rows - 16, DK), bf16),
        in_specs=[pl.BlockSpec(memory_space=pltpu.VMEM)] * 2,
        out_specs=pl.BlockSpec(memory_space=pltpu.VMEM),
        compiler_params=pltpu.CompilerParams(vmem_limit_bytes=24 * 1024 * 1024),
        cost_estimate=pl.CostEstimate(
            flops=4 * received.size, bytes_accessed=6 * received.size, transcendentals=0
        ),
    )(received_fade, received)


def outside_kernel(q_ref, k_ref, g_ref, inside_ref, state_ref, gate_ref, gain_ref, mixed_ref, gated_ref):
    for head in range(H):
        wide = slice(head * DV, (head + 1) * DV)
        c, e, qt, kt, kl = block_terms(q_ref, k_ref, g_ref, head)
        mixed = (inside_ref[:, wide] + fine(qt, state_ref[head], (1, 1))).astype(bf16)
        mixed_ref[:, wide] = mixed
        m = mixed.astype(f32)
        gate = gate_ref[:, wide]
        scale = lax.rsqrt(jnp.maximum(jnp.mean(m * m, axis=1, keepdims=True), head_floor))
        gated_ref[:, wide] = (m * scale * gain_ref[...] * (gate * jax.nn.sigmoid(gate))).astype(bf16)


def back_state_kernel(
    q_ref, k_ref, g_ref, dy_ref, mixed_ref, gate_ref, gain_ref,
    d_mixed_ref, d_gate_ref, gain_grad_ref, send_ref,
):
    gain_grad = jnp.zeros((1, DV), f32)
    gain = gain_ref[...]
    for head in range(H):
        wide = slice(head * DV, (head + 1) * DV)
        c, e, qt, kt, kl = block_terms(q_ref, k_ref, g_ref, head)
        m = mixed_ref[:, wide].astype(f32)
        gate = gate_ref[:, wide]
        dy = dy_ref[:, wide]
        square = jnp.mean(m * m, axis=1, keepdims=True)
        scale = lax.rsqrt(jnp.maximum(square, head_floor))
        sig = jax.nn.sigmoid(gate)
        silu = gate * sig
        unit = m * scale
        d_gate_ref[:, wide] = (dy * unit * gain * (sig * (1.0 + gate * (1.0 - sig)))).astype(bf16)
        d_normed = dy * silu
        gain_grad = gain_grad + jnp.sum(d_normed * unit, axis=0, keepdims=True)
        t = d_normed * gain
        inner = jnp.sum(t * m, axis=1, keepdims=True) * (1.0 / DV)
        share = jnp.where(square > head_floor, 1.0, jnp.where(square == head_floor, 0.5, 0.0))
        d_mixed = (t * scale - m * (inner * share * scale * scale * scale)).astype(bf16)
        d_mixed_ref[:, wide] = d_mixed
        store_groups(send_ref, head, fine(d_mixed, qt, (0, 0)))
    gain_grad_ref[0] = jnp.broadcast_to(gain_grad, (8, DV)) * 0.125


def back_kernel(
    q_ref, k_ref, g_ref, v_ref, do_ref, state_ref, after_ref, dq_ref, dk_ref, dg_ref, dv_ref
):
    mask = triangle()
    upper = jnp.where(
        lax.broadcasted_iota(jnp.int32, (SPAN, SPAN), 0)
        <= lax.broadcasted_iota(jnp.int32, (SPAN, SPAN), 1),
        1.0,
        0.0,
    ).astype(bf16)
    last = lax.broadcasted_iota(jnp.int32, (SPAN, DK), 0) == SPAN - 1
    for head in range(H):
        wide = slice(head * DV, (head + 1) * DV)
        cols = slice(head * DK, (head + 1) * DK)
        c, e, qt, kt, kl = block_terms(q_ref, k_ref, g_ref, head)
        v = v_ref[:, wide]
        do = do_ref[:, wide]
        state = state_ref[head]
        after = after_ref[head]
        scores = jnp.where(mask, fine(qt, kt, (1, 1)), 0.0)
        d_scores = jnp.where(mask, fine(do, v, (1, 1)), 0.0)
        dv_ref[:, wide] = (fine(scores, do, (0, 0)) + fine(kl, after, (1, 1))).astype(bf16)
        dqt = fine(d_scores, kt, (1, 0)) + fine(do, state, (1, 0))
        dkt = fine(d_scores, qt, (0, 0))
        dkl = fine(v, after, (1, 0))
        dq_ref[:, cols] = (dqt * (DK ** (-0.5) * jnp.exp(c))).astype(bf16)
        dk_ref[:, cols] = (dkt * jnp.exp(-c) + dkl * jnp.exp(e - c)).astype(bf16)
        tail = kl * dkl
        fade_grad = jnp.sum(after.astype(f32) * state.astype(f32), axis=0, keepdims=True)
        de = jnp.sum(tail, axis=0, keepdims=True) + jnp.exp(e) * fade_grad
        dc = qt * dqt - kt * dkt - tail + jnp.where(last, de, 0.0)
        dg_ref[:, cols] = fine(upper, dc, (1, 0)).astype(bf16)


def row_spec(width):
    return pl.BlockSpec((SPAN, width), lambda i: (i, 0))


def state_spec(groups, count):
    return pl.BlockSpec((H, groups, count, DK), lambda i: (i, 0, 0, 0))


def block_call(kernel, seq_count, in_specs, out_specs, out_shape, flops):
    return pl.pallas_call(
        kernel,
        grid=(seq_count,),
        in_specs=in_specs,
        out_specs=out_specs,
        out_shape=out_shape,
        compiler_params=pltpu.CompilerParams(vmem_limit_bytes=24 * 1024 * 1024),
        cost_estimate=pl.CostEstimate(
            flops=flops * seq_count * H, bytes_accessed=4 * 1024 * 1024, transcendentals=0
        ),
    )


class Links:
    def __init__(self):
        self.fsdp = lax.axis_index("fsdp")
        self.seq = lax.axis_index("seq")
        self.seq_count = lax.axis_size("seq")
        self.bits = self.seq_count.bit_length() - 1

    def own(self, axis):
        return self.fsdp if axis == "fsdp" else lax.rem(lax.div(self.seq, 1 << axis), 2)

    def swap_by_core(self, array, axes):
        if axes[0] == axes[1]:
            return self.swap(array, axes[0])
        count, moves = self.seq_count, []
        for fsdp in range(2):
            for seq in range(count):
                axis = axes[seq % 2]
                to = (1 - fsdp, seq) if axis == "fsdp" else (fsdp, seq ^ (1 << axis))
                moves.append((fsdp * count + seq, to[0] * count + to[1]))
        return lax.ppermute(array, ("fsdp", "seq"), moves)

    def by_core(self, pair):
        return jnp.where(self.own(0) == 0, pair[0], pair[1])

    def swap(self, array, axis):
        if axis == "fsdp":
            return lax.ppermute(array, "fsdp", [(0, 1), (1, 0)])
        return lax.ppermute(
            array, "seq", [(i, i ^ (1 << axis)) for i in range(self.seq_count)]
        )


def pick(array, index, axis=0):
    return lax.dynamic_index_in_dim(array, index, axis, keepdims=False)


def in_order(bit, own, other, axis):
    size = own.shape[axis]
    shape = list(own.shape)
    shape[axis] = 2 * size
    whole = jnp.zeros(shape, own.dtype)
    whole = lax.dynamic_update_slice_in_dim(whole, own, bit * size, axis)
    return lax.dynamic_update_slice_in_dim(whole, other, (1 - bit) * size, axis)


def own_piece(links, array, bit):
    rows = array.shape[0] // 4
    place = links.own(0) * 2 + links.own(bit)
    return lax.dynamic_slice_in_dim(array, place * rows, rows, 0)


def core_half(links, array):
    rows = array.shape[0] // 2
    return lax.dynamic_slice_in_dim(array, links.own(0) * rows, rows, 0)


def lay_down(links, *arrays):
    rows = arrays[0].shape[0]
    whole = jnp.zeros((2 * rows, sum(array.shape[1] for array in arrays)), bf16)
    col = 0
    for array in arrays:
        whole = lax.dynamic_update_slice(whole, array, (links.fsdp * rows, col))
        col += array.shape[1]
    return whole


def fill_other(links, whole, near, far):
    rows = whole.shape[0] // 2
    base = (1 - links.fsdp) * rows
    core = links.own(0)
    whole = lax.dynamic_update_slice(whole, near, (base + core * (rows // 2), 0))
    return lax.dynamic_update_slice(whole, far, (base + (1 - core) * (rows // 2), 0))


def feed_kernel(
    place_ref, norm_ref, dy_ref, gate_own, gate_near, gate_far, up_own, up_near, up_far, down_ref,
    hidden_ref, d_gate_ref, d_up_ref, final_ref, d_norm_ref,
):
    @pl.when(pl.program_id(0) == 0)
    def _():
        final_ref[...] = jnp.zeros_like(final_ref)
        d_norm_ref[...] = jnp.zeros_like(d_norm_ref)

    parts = []
    for i, (gate_part, up_part) in enumerate(
        ((gate_own, up_own), (gate_near, up_near), (gate_far, up_far))
    ):
        rows = gate_part.shape[0]
        parts.append((pl.ds(pl.multiple_of(place_ref[i], rows), rows), gate_part, up_part))
    gate = sum(dot(norm_ref[:, spot], part[...], (1, 0)) for spot, part, _ in parts)
    up = sum(dot(norm_ref[:, spot], part[...], (1, 0)) for spot, _, part in parts)
    down = down_ref[...]
    d_hidden = dot(dy_ref[...], down, (1, 1))
    sig = jax.nn.sigmoid(gate)
    silu = gate * sig
    hidden = (silu * up).astype(bf16)
    d_gate = (d_hidden * up * (sig * (1.0 + gate * (1.0 - sig)))).astype(bf16)
    d_up = (d_hidden * silu).astype(bf16)
    hidden_ref[...] = hidden
    d_gate_ref[...] = d_gate
    d_up_ref[...] = d_up
    final_ref[...] += dot(hidden, down, (1, 0))
    for spot, gate_part, up_part in parts:
        d_norm_ref[:, spot] += dot(d_gate, gate_part[...], (1, 1)) + dot(d_up, up_part[...], (1, 1))


def feed_forward(places, norm, dy, gates, ups, down):
    rows, width = norm.shape
    hidden_width = down.shape[0]
    block = 256
    still = lambda shape: pl.BlockSpec(shape, lambda j: (0, 0))
    along = lambda height: pl.BlockSpec((height, block), lambda j: (0, j))
    return pl.pallas_call(
        feed_kernel,
        grid=(hidden_width // block,),
        in_specs=[pl.BlockSpec(memory_space=pltpu.SMEM), still((rows, width)), still((rows, width))]
        + [along(part.shape[0]) for part in (*gates, *ups)]
        + [pl.BlockSpec((block, width), lambda j: (j, 0))],
        out_specs=[along(rows)] * 3 + [still((rows, width))] * 2,
        out_shape=[jax.ShapeDtypeStruct((rows, hidden_width), bf16)] * 3
        + [jax.ShapeDtypeStruct((rows, width), f32)] * 2,
        compiler_params=pltpu.CompilerParams(vmem_limit_bytes=36 * 1024 * 1024),
        cost_estimate=pl.CostEstimate(
            flops=12 * rows * width * hidden_width,
            bytes_accessed=6 * width * hidden_width,
            transcendentals=rows * hidden_width,
        ),
    )(places, norm, dy, *gates, *ups, down)


class Share:
    def __init__(self, links, partial, widths, halving, doubling):
        self.links, self.widths = links, widths
        groups, rows, self.cols = partial.shape
        self.rows = rows
        far = [("meet", (axis, axis)) for axis in range(3, links.bits)]
        self.steps = [("halve", axes) for axes in zip(*halving)] + far
        self.steps += [("double", axes) for axes in zip(*doubling)] + [("core", (0, 0))]
        self.left = (["fsdp", 1, 2], ["fsdp", 1, 2])
        self.data = partial.reshape((groups, 2, 2, 2, rows // 8, self.cols))
        self.outs = self.pending = None

    def cut(self, axes, other):
        links = self.links
        bits = [links.own(axis) for axis in axes]
        if other:
            bits = [1 - bit for bit in bits]
        dims = [1 + left.index(axis) for left, axis in zip(self.left, axes)]
        if dims[0] == dims[1]:
            return pick(self.data, bits[0] if axes[0] == axes[1] else links.by_core(bits), dims[0])
        return links.by_core([pick(self.data, bit, dim) for bit, dim in zip(bits, dims)])

    def receive(self, hold):
        if self.pending is None:
            return
        kind, axes, got = self.pending
        self.pending = None
        links, got = self.links, hold(got)
        if kind == "halve":
            kept = self.cut(axes, False)
            self.data = (kept.astype(f32) + got.astype(f32)).astype(bf16)
            for left, axis in zip(self.left, axes):
                left.remove(axis)
        elif kind == "meet":
            self.data = (self.data.astype(f32) + got.astype(f32)).astype(bf16)
        elif kind == "double":
            bits = [links.own(axis) for axis in axes]
            bit = bits[0] if axes[0] == axes[1] else links.by_core(bits)
            dims = [1 + sum(1 for o in left if o < axis) for left, axis in zip(self.left, axes)]
            data = in_order(bit, jnp.expand_dims(self.data, 1), jnp.expand_dims(got, 1), 1)
            moved = [jnp.moveaxis(data, 1, dim) for dim in dims]
            self.data = moved[0] if dims[0] == dims[1] else links.by_core(moved)
            for left, axis, dim in zip(self.left, axes, dims):
                left.insert(dim - 1, axis)
        else:
            shape = (self.data.shape[0], self.rows // 2, self.cols)
            own, other = self.data.reshape(shape), got.reshape(shape)
            self.outs = [
                out
                for i, widths in enumerate(self.widths)
                for out in finish_columns(self.links, own[i], other[i], widths)
            ]

    def step(self, after_last, hold):
        self.receive(after_last)
        kind, axes = self.steps.pop(0)
        send = self.cut(axes, True) if kind == "halve" else self.data
        got = self.links.swap_by_core(hold(send), axes)
        self.pending = (kind, axes, got)
        return got


def finish_kernel(widths, first_ref, own_ref, other_ref, *out_refs):
    first = first_ref[0] == 0
    low = jnp.where(first, own_ref[...], other_ref[...]).astype(f32)
    high = jnp.where(first, other_ref[...], own_ref[...]).astype(f32)
    offset = 0
    for width, out_ref in zip(widths, out_refs):
        half = width // 2
        out_ref[:, :half] = low[:, offset : offset + half]
        out_ref[:, half:] = high[:, offset : offset + half]
        offset += half


def finish_columns(links, own, other, widths):
    rows, cols = own.shape
    block = rows // 4
    spec = pl.BlockSpec((block, cols), lambda i: (i, 0))
    outs = pl.pallas_call(
        functools.partial(finish_kernel, widths),
        grid=(4,),
        in_specs=[pl.BlockSpec(memory_space=pltpu.SMEM), spec, spec],
        out_specs=[pl.BlockSpec((block, width), lambda i: (i, 0)) for width in widths],
        out_shape=[jax.ShapeDtypeStruct((rows, width), f32) for width in widths],
        compiler_params=pltpu.CompilerParams(vmem_limit_bytes=28 * 1024 * 1024),
        cost_estimate=pl.CostEstimate(flops=0, bytes_accessed=12 * own.size, transcendentals=0),
    )(links.own(0).reshape(1).astype(jnp.int32), own, other)
    return list(outs)


def half_columns(links, array, parts):
    mine = links.own(0)
    ours, theirs = [], []
    offset = 0
    for width in parts:
        piece = array[:, offset : offset + width]
        ours.append(lax.dynamic_slice_in_dim(piece, mine * (width // 2), width // 2, 1))
        theirs.append(lax.dynamic_slice_in_dim(piece, (1 - mine) * (width // 2), width // 2, 1))
        offset += width
    return join(ours), join(theirs)


def join(arrays):
    return arrays[0] if len(arrays) == 1 else jnp.concatenate(arrays, axis=1)


def with_other_core(links, ours, theirs):
    got = links.swap(join(theirs), 0)
    offset, outs = 0, []
    for array in ours:
        width = array.shape[1]
        outs.append(jnp.concatenate((array, got[:, offset : offset + width]), axis=0))
        offset += width
    return outs


def fence(*arrays):
    return lax.optimization_barrier(arrays)


def per_device(
    inputs,
    mixer_gain,
    query_weight,
    key_weight,
    value_weight,
    decay_down,
    decay_up,
    decay_bias,
    outgate_weight,
    head_gain,
    output_weight,
    feed_gain,
    feed_gate,
    feed_up,
    feed_down,
    cotangent,
):
    links = Links()
    seq_count, seg_rows, width = inputs.shape
    row_count = seq_count * seg_rows
    hidden_width = feed_gate.shape[1]
    key_cols, value_cols = H * DK, H * DV
    groups = links.seq_count // (seq_count * H)
    state_rows = DV // groups

    in_weights = (query_weight, key_weight, value_weight, outgate_weight)
    in_widths = (key_cols, key_cols, value_cols, value_cols)
    core = links.own(0)
    piece_in = join([core_half(links, weight) for weight in in_weights])
    near_in = links.swap(piece_in, "fsdp")
    piece_gate, piece_up = own_piece(links, feed_gate, 1), core_half(links, feed_up)
    piece_out = jnp.concatenate(
        (own_piece(links, feed_down, 1), own_piece(links, output_weight, 1)), axis=0
    )
    out_rows = (feed_down.shape[0] // 4, output_weight.shape[0] // 4)
    mine1 = links.own(1)
    full_in = lay_down(links, *in_weights)

    small = (mixer_gain, decay_down, decay_up, decay_bias, head_gain, feed_gain)
    packed = jnp.concatenate([piece.reshape(-1) for piece in small])
    packed_other = links.swap(packed, "fsdp")

    far_in = links.swap(near_in, 0)
    y_out = links.swap(fence(piece_out, near_in, full_in)[0], "fsdp")
    full_in = fill_other(links, full_in, near_in, far_in)

    low_half = jnp.where(links.fsdp == 0, packed, packed_other)
    high_half = jnp.where(links.fsdp == 0, packed_other, packed)
    whole_small = []
    offset = 0
    for piece in small:
        parts = [half[offset : offset + piece.size].reshape(piece.shape) for half in (low_half, high_half)]
        whole_small.append(jnp.concatenate(parts, axis=0))
        offset += piece.size
    full_mixer_gain, full_down, full_up_rank, full_bias, full_head_gain, full_feed_gain = whole_small
    head_gain_row = full_head_gain.astype(f32).reshape(1, DV)

    residual_in = inputs.reshape(row_count, width).astype(f32)
    normed_full, first_pull = jax.vjp(rms_scale, residual_in, full_mixer_gain.astype(f32))
    normed = normed_full.astype(bf16)
    projected = mat_product(normed, full_in)
    query = projected[:, :key_cols].astype(bf16)
    keys = projected[:, key_cols : 2 * key_cols].astype(bf16)
    values = projected[:, 2 * key_cols : 2 * key_cols + value_cols].astype(bf16)
    out_gate = projected[:, 2 * key_cols + value_cols :]
    ranked = mat_product(normed, full_down).astype(bf16)
    decay_in = mat_product(ranked, full_up_rank) + full_bias.astype(f32)
    decay = (jax.nn.log_sigmoid(decay_in) / gate_scale).astype(bf16)

    qkg_specs = [row_spec(key_cols)] * 3
    rows_wide = row_spec(value_cols)
    gain_spec = pl.BlockSpec((1, DV), lambda i: (0, 0))
    whole_state = pl.BlockSpec((H, DV, DK), lambda i: (i, 0, 0))
    wide_shape = jax.ShapeDtypeStruct((row_count, value_cols), bf16)
    block_flops = 2 * SPAN * DK * DV * 6

    def to_heads(array):
        rows = array.shape[2]
        return lax.all_to_all(
            array.reshape(links.seq_count, rows, DK), "seq", split_axis=0, concat_axis=0, tiled=True
        )

    def to_tokens(array):
        back = lax.all_to_all(array, "seq", split_axis=0, concat_axis=0, tiled=True)
        return back.reshape(seq_count * H, DV, DK)

    inside, update = block_call(
        local_kernel,
        seq_count,
        qkg_specs + [rows_wide],
        [rows_wide, state_spec(groups, state_rows + 16)],
        [
            jax.ShapeDtypeStruct((row_count, value_cols), f32),
            jax.ShapeDtypeStruct((seq_count * H, groups, state_rows + 16, DK), bf16),
        ],
        2 * block_flops,
    )(query, keys, decay, values)
    y_gate = links.swap(fence(piece_gate, y_out, update)[0], "fsdp")
    near_up = links.swap(fence(piece_up, y_gate)[0], "fsdp")
    y_out = fence(y_out, update)[0]
    x_out = links.swap(y_out, 1)
    x_gate = links.swap(y_gate, 1)
    received = to_heads(update)
    before = scan_blocks(False, received, received)
    near_up, x_gate = fence(near_up, before)[0], fence(x_gate, before)[0]
    full_feed_down = lay_down(links, fence(feed_down, update)[0])
    full_output = lay_down(links, fence(output_weight, update)[0])
    near_down = in_order(mine1, y_out[: out_rows[0]], x_out[: out_rows[0]], 0)
    near_output = in_order(mine1, y_out[out_rows[0] :], x_out[out_rows[0] :], 0)
    far_out = links.swap(jnp.concatenate((near_down, near_output), axis=0), 0)
    far_down, far_output = far_out[: 2 * out_rows[0]], far_out[2 * out_rows[0] :]
    full_feed_down = fill_other(links, full_feed_down, near_down, far_down)
    full_output = fill_other(links, full_output, near_output, far_output)
    near_gate = in_order(mine1, y_gate, x_gate, 0)
    far_gate = links.swap(near_gate, 0)
    far_up = links.swap(near_up, 0)
    d_down = cotangent.reshape(row_count, width)
    seq_grad = d_down.astype(f32)
    down_ours, down_theirs = half_columns(links, d_down, (width,))
    normed_both, down_both = with_other_core(
        links, (normed, down_ours), (fence(normed, update)[0], down_theirs)
    )
    state = to_tokens(before)
    mixed, gated = block_call(
        outside_kernel,
        seq_count,
        qkg_specs + [rows_wide, whole_state, rows_wide, gain_spec],
        [rows_wide] * 2,
        [wide_shape] * 2,
        block_flops,
    )(query, keys, decay, inside, state, out_gate, head_gain_row)


    middle = residual_in + mat_product(gated, full_output)
    second_full, second_pull = jax.vjp(rms_scale, middle, full_feed_gain.astype(f32))
    second_norm = second_full.astype(bf16)
    half = width // 2
    other_base = (1 - links.fsdp) * half
    places = jnp.stack(
        (links.fsdp * half, other_base + core * (half // 2), other_base + (1 - core) * (half // 2))
    ).astype(jnp.int32)
    hidden, d_gate, d_up, fed, d_second = feed_forward(
        places,
        second_norm,
        d_down,
        (feed_gate, near_gate, far_gate),
        (feed_up, near_up, far_up),
        full_feed_down,
    )
    output = (middle + fed).astype(bf16).reshape(seq_count, seg_rows, width)

    (second_both,) = with_other_core(links, (second_norm,), (second_norm,))
    (hidden_both,) = with_other_core(links, (hidden,), (hidden,))
    grad_down = cross_rows(hidden_both, down_both).astype(bf16)

    x, y, z = 1, "fsdp", 2
    cuts = (([y, x, z], [x, z, y]), ([y, z, x], [z, x, y]), ([y, x, z], [y, z, x]))
    joins = ([z, x], [x, z])
    shares, arrived, sent, extras = {}, [], [], []

    def after_last(array):
        return fence(array, *sent[-1:])[0]

    def hold(array, *due):
        behind = (*arrived[-4:-3], *sent[-1:], *extras, *due)
        sent.append(array)
        return fence(array, *behind)[0]

    def go(*names):
        for name in names:
            share = shares[name]
            if not share.steps:
                share.receive(after_last)
                sent.append(share.outs[0])
                continue
            arrived.append(share.step(after_last, hold))
            while share.steps and share.steps[0][0] == "meet" and share.steps[0][1][0] > 3:
                arrived.append(share.step(after_last, hold))

    shares["down"] = Share(links, grad_down[None], [(width,)], cuts[0], joins)
    go("down")
    d_second = fence(d_second, sent[0])[0]

    gate_ours, gate_theirs = half_columns(links, d_gate, (hidden_width,))
    up_ours, up_theirs = half_columns(links, d_up, (hidden_width,))
    gate_both, up_both = with_other_core(links, (gate_ours, up_ours), (gate_theirs, up_theirs))
    grad_gate = cross_rows(second_both, gate_both).astype(bf16)
    grad_up = cross_rows(second_both, up_both).astype(bf16)

    d_middle_norm, grad_feed_gain = second_pull(d_second)
    d_middle = seq_grad + d_middle_norm
    d_branch = d_middle.astype(bf16)
    d_gated = back_product(d_branch, full_output)
    d_mixed, d_outgate, gain_parts, back_update = block_call(
        back_state_kernel,
        seq_count,
        qkg_specs + [rows_wide] * 3 + [gain_spec],
        [rows_wide] * 2
        + [pl.BlockSpec((1, 8, DV), lambda i: (i, 0, 0)), state_spec(groups, state_rows)],
        [wide_shape] * 2
        + [
            jax.ShapeDtypeStruct((seq_count, 8, DV), f32),
            jax.ShapeDtypeStruct((seq_count * H, groups, state_rows, DK), bf16),
        ],
        block_flops,
    )(query, keys, decay, d_gated, mixed, out_gate, head_gain_row)
    grad_head_gain = jnp.sum(gain_parts, axis=(0, 1))
    branch_ours, branch_theirs = half_columns(links, d_branch, (width,))
    outgate_ours, outgate_theirs = half_columns(links, d_outgate, (value_cols,))
    gated_both, branch_both, outgate_both = with_other_core(
        links, (gated, branch_ours, outgate_ours), (gated, branch_theirs, outgate_theirs)
    )
    grad_mixer_out = fence(
        jnp.stack(
            (
                cross_rows(gated_both, branch_both).astype(bf16),
                cross_rows(normed_both, outgate_both).astype(bf16),
            )
        )
    )[0]

    back_received = to_heads(hold(back_update))
    shares["gate"] = Share(links, grad_gate[None], [(hidden_width,)], cuts[1], joins)
    shares["out"] = Share(links, grad_mixer_out, [(width,), (value_cols,)], cuts[0], joins)
    shares["up"] = Share(links, grad_up[None], [(hidden_width,)], cuts[2], joins)
    go("gate", "out", "down")
    after = to_tokens(hold(scan_blocks(True, received, after_last(back_received))))
    go("up", "gate", "down")
    after = after_last(after)
    d_query, d_keys, d_decay, d_values = block_call(
        back_kernel,
        seq_count,
        qkg_specs + [rows_wide] * 2 + [whole_state] * 2,
        [row_spec(key_cols)] * 3 + [rows_wide],
        [jax.ShapeDtypeStruct((row_count, key_cols), bf16)] * 3 + [wide_shape],
        4 * block_flops,
    )(query, keys, decay, values, d_mixed, state, after)
    d_qkv = jnp.concatenate((d_query, d_keys, d_values), axis=1)
    qkv_ours, qkv_theirs = half_columns(links, d_qkv, in_widths[:3])
    (qkv_both,) = with_other_core(links, (qkv_ours,), (qkv_theirs,))
    grad_qkv = cross_rows(normed_both, qkv_both).astype(bf16)
    shares["qkv"] = Share(links, grad_qkv[None], [in_widths[:3]], cuts[1], joins)
    sent.append(d_query)
    go("qkv")
    d_qkv, d_decay, _ = fence(d_qkv, d_decay, sent[-1])

    d_decay_in = d_decay.astype(f32) * jax.nn.sigmoid(-decay_in) / gate_scale
    grad_decay_bias = jnp.sum(d_decay_in, axis=0)
    grad_decay_up = lax.dot_general(
        ranked.astype(f32), d_decay_in, (((0,), (0,)), ((), ())), precision=highest
    )
    d_ranked = lax.dot_general(
        d_decay_in, full_up_rank.astype(f32), (((1,), (1,)), ((), ())), precision=highest
    ).astype(bf16)
    grad_decay_down = cross_rows(normed, d_ranked)
    d_normed = back_product(
        jnp.concatenate((d_qkv, d_outgate), axis=1), full_in
    ) + back_product(d_ranked, full_down)
    d_input_norm, grad_mixer_gain = first_pull(d_normed)
    input_grad = (d_middle + d_input_norm).reshape(seq_count, seg_rows, width)

    small_grads = (
        grad_mixer_gain, grad_decay_down, grad_decay_up, grad_decay_bias, grad_head_gain,
        grad_feed_gain,
    )
    total = jnp.concatenate([grad.reshape(2, -1) for grad in small_grads], axis=1)
    go("up", "gate", "down", "out")
    other = links.swap(hold(pick(total, 1 - links.fsdp), input_grad, output), "fsdp")
    go("up", "qkv", "gate")
    total = (pick(total, links.fsdp) + after_last(other)).reshape(links.seq_count, -1)
    pieces = lax.all_to_all(hold(total), "seq", split_axis=0, concat_axis=0, tiled=True)
    go("out", "qkv", "up", "gate")
    own_sum = jnp.sum(after_last(pieces), axis=0, keepdims=True)
    own_sum = hold(jnp.broadcast_to(own_sum, total.shape))
    total = lax.all_to_all(own_sum, "seq", split_axis=0, concat_axis=0, tiled=True)
    go("down", "out", "up", "down", "qkv", "gate")
    total = after_last(total).reshape(-1)
    small_out = []
    offset = 0
    for grad in small_grads:
        size = grad.size // 2
        small_out.append(
            total[offset : offset + size].reshape((grad.shape[0] // 2,) + grad.shape[1:])
        )
        offset += size
    out_mixer_gain, out_decay_down, out_decay_up, out_bias, out_head_gain, out_feed_gain = small_out
    extras.extend(small_out)
    go("qkv", "out", "up", "down", "qkv", "down", "out", "gate", "qkv", "up", "gate", "out", "qkv", "up", "out")
    results = [
        out for name in ("down", "gate", "up", "out", "qkv") for out in shares[name].outs
    ]


    (
        out_down, out_gate_w, out_up_w, out_output, out_outgate, out_query, out_key, out_value,
    ) = results
    return (
        output,
        input_grad,
        out_mixer_gain,
        out_query,
        out_key,
        out_value,
        out_decay_down,
        out_decay_up,
        out_bias,
        out_outgate,
        out_head_gain,
        out_output,
        out_feed_gain,
        out_gate_w,
        out_up_w,
        out_down,
    )


def solution(mesh):
    rows = P("fsdp", None)
    gains = P("fsdp")
    tokens = P("fsdp", "seq", None)
    weights = (gains, rows, rows, rows, rows, rows, gains, rows, gains, rows, gains, rows, rows, rows)
    return jax.shard_map(
        per_device,
        mesh=mesh,
        in_specs=(tokens,) + weights + (tokens,),
        out_specs=(tokens, tokens) + weights,
        check_vma=False,
    )
```

```python
import functools

import jax
import jax.numpy as jnp
from jax import lax
from jax.experimental import pallas as pl
from jax.experimental.pallas import tpu as pltpu
from jax.sharding import PartitionSpec as P

H = 4
DK = 128
DV = 256
SPAN = 64


epsilon = 1e-06
head_floor = 0.25
gate_scale = 16.0
highest = lax.Precision.HIGHEST
bf16 = jnp.bfloat16
f32 = jnp.float32


def rms_scale(values, scale_gain):
    return (
        values * lax.rsqrt(jnp.mean(values * values, axis=-1, keepdims=True) + epsilon) * scale_gain
    )


def mat_product(left, right):
    return jnp.dot(left, right, preferred_element_type=f32)


def cross_rows(left, right):
    return lax.dot_general(left, right, (((0,), (0,)), ((), ())), preferred_element_type=f32)


def back_product(left, right):
    return lax.dot_general(left, right, (((1,), (1,)), ((), ())), preferred_element_type=f32)


def dot(left, right, contract):
    return lax.dot_general(
        left, right, (((contract[0],), (contract[1],)), ((), ())), preferred_element_type=f32
    )


def fine(left, right, contract):
    lefts, rights = parts_of(left), parts_of(right)
    total = dot(lefts[0], rights[0], contract)
    if len(lefts) > 1:
        total = total + dot(lefts[1], rights[0], contract)
    if len(rights) > 1:
        total = total + dot(lefts[0], rights[1], contract)
    return total


def parts_of(array):
    if array.dtype == bf16:
        return (array,)
    high = array.astype(bf16)
    return high, (array - high.astype(f32)).astype(bf16)


def triangle():
    rows = lax.broadcasted_iota(jnp.int32, (SPAN, SPAN), 0)
    cols = lax.broadcasted_iota(jnp.int32, (SPAN, SPAN), 1)
    return rows >= cols


def block_terms(q_ref, k_ref, g_ref, head):
    cols = slice(head * DK, (head + 1) * DK)
    lower = jnp.where(triangle(), 1.0, 0.0).astype(bf16)
    c = jnp.dot(lower, g_ref[:, cols], preferred_element_type=f32)
    e = c[SPAN - 1 : SPAN, :]
    qt = q_ref[:, cols].astype(f32) * DK ** (-0.5) * jnp.exp(c)
    keys = k_ref[:, cols].astype(f32)
    return c, e, qt, keys * jnp.exp(-c), keys * jnp.exp(e - c)


def store_groups(ref, head, state):
    groups, size = ref.shape[1], ref.shape[2]
    count = state.shape[0] // groups
    for group in range(groups):
        ref[head, group, 0:count, :] = state[group * count : (group + 1) * count, :].astype(bf16)


def local_kernel(q_ref, k_ref, g_ref, v_ref, inside_ref, send_ref):
    groups = send_ref.shape[1]
    count = DV // groups
    place = lax.broadcasted_iota(jnp.int32, (16, DK), 0)
    for head in range(H):
        wide = slice(head * DV, (head + 1) * DV)
        c, e, qt, kt, kl = block_terms(q_ref, k_ref, g_ref, head)
        v = v_ref[:, wide]
        scores = jnp.where(triangle(), fine(qt, kt, (1, 1)), 0.0)
        inside_ref[:, wide] = fine(scores, v, (1, 0))
        store_groups(send_ref, head, fine(v, kl, (0, 0)))
        fade = jnp.exp(e)
        high = fade.astype(bf16).astype(f32)
        tail = jnp.where(place == 0, high, jnp.where(place == 1, fade - high, 0.0)).astype(bf16)
        for group in range(groups):
            send_ref[head, group, count : count + 16, :] = tail


def scan_kernel(backward, fade_ref, update_ref, before_ref):
    blocks, count, _ = before_ref.shape

    def step(i, state):
        block = blocks - 1 - i if backward else i
        before_ref[block] = state.astype(bf16)
        tail = fade_ref[block, count : count + 16, :].astype(f32)
        fade = tail[0:1, :] + tail[1:2, :]
        return state * fade + update_ref[block, 0:count, :].astype(f32)

    lax.fori_loop(0, blocks, step, jnp.zeros((count, DK), f32), unroll=4)


def scan_blocks(backward, received_fade, received):
    blocks, rows, _ = received_fade.shape
    return pl.pallas_call(
        functools.partial(scan_kernel, backward),
        out_shape=jax.ShapeDtypeStruct((blocks, rows - 16, DK), bf16),
        in_specs=[pl.BlockSpec(memory_space=pltpu.VMEM)] * 2,
        out_specs=pl.BlockSpec(memory_space=pltpu.VMEM),
        compiler_params=pltpu.CompilerParams(vmem_limit_bytes=24 * 1024 * 1024),
        cost_estimate=pl.CostEstimate(
            flops=4 * received.size, bytes_accessed=6 * received.size, transcendentals=0
        ),
    )(received_fade, received)


def outside_kernel(q_ref, k_ref, g_ref, inside_ref, state_ref, gate_ref, gain_ref, mixed_ref, gated_ref):
    for head in range(H):
        wide = slice(head * DV, (head + 1) * DV)
        c, e, qt, kt, kl = block_terms(q_ref, k_ref, g_ref, head)
        mixed = (inside_ref[:, wide] + fine(qt, state_ref[head], (1, 1))).astype(bf16)
        mixed_ref[:, wide] = mixed
        m = mixed.astype(f32)
        gate = gate_ref[:, wide]
        scale = lax.rsqrt(jnp.maximum(jnp.mean(m * m, axis=1, keepdims=True), head_floor))
        gated_ref[:, wide] = (m * scale * gain_ref[...] * (gate * jax.nn.sigmoid(gate))).astype(bf16)


def back_state_kernel(
    q_ref, k_ref, g_ref, dy_ref, mixed_ref, gate_ref, gain_ref,
    d_mixed_ref, d_gate_ref, gain_grad_ref, send_ref,
):
    gain_grad = jnp.zeros((1, DV), f32)
    gain = gain_ref[...]
    for head in range(H):
        wide = slice(head * DV, (head + 1) * DV)
        c, e, qt, kt, kl = block_terms(q_ref, k_ref, g_ref, head)
        m = mixed_ref[:, wide].astype(f32)
        gate = gate_ref[:, wide]
        dy = dy_ref[:, wide]
        square = jnp.mean(m * m, axis=1, keepdims=True)
        scale = lax.rsqrt(jnp.maximum(square, head_floor))
        sig = jax.nn.sigmoid(gate)
        silu = gate * sig
        unit = m * scale
        d_gate_ref[:, wide] = (dy * unit * gain * (sig * (1.0 + gate * (1.0 - sig)))).astype(bf16)
        d_normed = dy * silu
        gain_grad = gain_grad + jnp.sum(d_normed * unit, axis=0, keepdims=True)
        t = d_normed * gain
        inner = jnp.sum(t * m, axis=1, keepdims=True) * (1.0 / DV)
        share = jnp.where(square > head_floor, 1.0, jnp.where(square == head_floor, 0.5, 0.0))
        d_mixed = (t * scale - m * (inner * share * scale * scale * scale)).astype(bf16)
        d_mixed_ref[:, wide] = d_mixed
        store_groups(send_ref, head, fine(d_mixed, qt, (0, 0)))
    gain_grad_ref[0] = jnp.broadcast_to(gain_grad, (8, DV)) * 0.125


def back_kernel(
    q_ref, k_ref, g_ref, v_ref, do_ref, state_ref, after_ref, dq_ref, dk_ref, dg_ref, dv_ref
):
    mask = triangle()
    upper = jnp.where(
        lax.broadcasted_iota(jnp.int32, (SPAN, SPAN), 0)
        <= lax.broadcasted_iota(jnp.int32, (SPAN, SPAN), 1),
        1.0,
        0.0,
    ).astype(bf16)
    last = lax.broadcasted_iota(jnp.int32, (SPAN, DK), 0) == SPAN - 1
    for head in range(H):
        wide = slice(head * DV, (head + 1) * DV)
        cols = slice(head * DK, (head + 1) * DK)
        c, e, qt, kt, kl = block_terms(q_ref, k_ref, g_ref, head)
        v = v_ref[:, wide]
        do = do_ref[:, wide]
        state = state_ref[head]
        after = after_ref[head]
        scores = jnp.where(mask, fine(qt, kt, (1, 1)), 0.0)
        d_scores = jnp.where(mask, fine(do, v, (1, 1)), 0.0)
        dv_ref[:, wide] = (fine(scores, do, (0, 0)) + fine(kl, after, (1, 1))).astype(bf16)
        dqt = fine(d_scores, kt, (1, 0)) + fine(do, state, (1, 0))
        dkt = fine(d_scores, qt, (0, 0))
        dkl = fine(v, after, (1, 0))
        dq_ref[:, cols] = (dqt * (DK ** (-0.5) * jnp.exp(c))).astype(bf16)
        dk_ref[:, cols] = (dkt * jnp.exp(-c) + dkl * jnp.exp(e - c)).astype(bf16)
        tail = kl * dkl
        fade_grad = jnp.sum(after.astype(f32) * state.astype(f32), axis=0, keepdims=True)
        de = jnp.sum(tail, axis=0, keepdims=True) + jnp.exp(e) * fade_grad
        dc = qt * dqt - kt * dkt - tail + jnp.where(last, de, 0.0)
        dg_ref[:, cols] = fine(upper, dc, (1, 0)).astype(bf16)


def row_spec(width):
    return pl.BlockSpec((SPAN, width), lambda i: (i, 0))


def state_spec(groups, count):
    return pl.BlockSpec((H, groups, count, DK), lambda i: (i, 0, 0, 0))


def block_call(kernel, seq_count, in_specs, out_specs, out_shape, flops):
    return pl.pallas_call(
        kernel,
        grid=(seq_count,),
        in_specs=in_specs,
        out_specs=out_specs,
        out_shape=out_shape,
        compiler_params=pltpu.CompilerParams(vmem_limit_bytes=24 * 1024 * 1024),
        cost_estimate=pl.CostEstimate(
            flops=flops * seq_count * H, bytes_accessed=4 * 1024 * 1024, transcendentals=0
        ),
    )


class Links:
    def __init__(self):
        self.fsdp = lax.axis_index("fsdp")
        self.seq = lax.axis_index("seq")
        self.seq_count = lax.axis_size("seq")
        self.bits = self.seq_count.bit_length() - 1

    def own(self, axis):
        return self.fsdp if axis == "fsdp" else lax.rem(lax.div(self.seq, 1 << axis), 2)

    def swap_by_core(self, array, axes):
        if axes[0] == axes[1]:
            return self.swap(array, axes[0])
        count, moves = self.seq_count, []
        for fsdp in range(2):
            for seq in range(count):
                axis = axes[seq % 2]
                to = (1 - fsdp, seq) if axis == "fsdp" else (fsdp, seq ^ (1 << axis))
                moves.append((fsdp * count + seq, to[0] * count + to[1]))
        return lax.ppermute(array, ("fsdp", "seq"), moves)

    def by_core(self, pair):
        return jnp.where(self.own(0) == 0, pair[0], pair[1])

    def swap(self, array, axis):
        if axis == "fsdp":
            return lax.ppermute(array, "fsdp", [(0, 1), (1, 0)])
        return lax.ppermute(
            array, "seq", [(i, i ^ (1 << axis)) for i in range(self.seq_count)]
        )


def pick(array, index, axis=0):
    return lax.dynamic_index_in_dim(array, index, axis, keepdims=False)


def in_order(bit, own, other, axis):
    size = own.shape[axis]
    shape = list(own.shape)
    shape[axis] = 2 * size
    whole = jnp.zeros(shape, own.dtype)
    whole = lax.dynamic_update_slice_in_dim(whole, own, bit * size, axis)
    return lax.dynamic_update_slice_in_dim(whole, other, (1 - bit) * size, axis)


def own_piece(links, array):
    rows = array.shape[0] // 4
    bit = links.by_core([links.own(axis) for axis in near_bits])
    return lax.dynamic_slice_in_dim(array, (links.own(0) * 2 + bit) * rows, rows, 0)


near_bits = (1, 2)


def near_half(links, own, other):
    return in_order(links.by_core([links.own(axis) for axis in near_bits]), own, other, 0)


def core_half(links, array):
    rows = array.shape[0] // 2
    return lax.dynamic_slice_in_dim(array, links.own(0) * rows, rows, 0)


def lay_down(links, *arrays):
    rows = arrays[0].shape[0]
    whole = jnp.zeros((2 * rows, sum(array.shape[1] for array in arrays)), bf16)
    col = 0
    for array in arrays:
        whole = lax.dynamic_update_slice(whole, array, (links.fsdp * rows, col))
        col += array.shape[1]
    return whole


def fill_other(links, whole, near, far):
    rows = whole.shape[0] // 2
    base = (1 - links.fsdp) * rows
    core = links.own(0)
    whole = lax.dynamic_update_slice(whole, near, (base + core * (rows // 2), 0))
    return lax.dynamic_update_slice(whole, far, (base + (1 - core) * (rows // 2), 0))


def feed_kernel(
    place_ref, norm_ref, dy_ref, gate_own, gate_near, gate_far, up_own, up_near, up_far, down_ref,
    hidden_ref, d_gate_ref, d_up_ref, final_ref, d_norm_ref,
):
    @pl.when(pl.program_id(0) == 0)
    def _():
        final_ref[...] = jnp.zeros_like(final_ref)
        d_norm_ref[...] = jnp.zeros_like(d_norm_ref)

    parts = []
    for i, (gate_part, up_part) in enumerate(
        ((gate_own, up_own), (gate_near, up_near), (gate_far, up_far))
    ):
        rows = gate_part.shape[0]
        parts.append((pl.ds(pl.multiple_of(place_ref[i], rows), rows), gate_part, up_part))
    gate = sum(dot(norm_ref[:, spot], part[...], (1, 0)) for spot, part, _ in parts)
    up = sum(dot(norm_ref[:, spot], part[...], (1, 0)) for spot, _, part in parts)
    down = down_ref[...]
    d_hidden = dot(dy_ref[...], down, (1, 1))
    sig = jax.nn.sigmoid(gate)
    silu = gate * sig
    hidden = (silu * up).astype(bf16)
    d_gate = (d_hidden * up * (sig * (1.0 + gate * (1.0 - sig)))).astype(bf16)
    d_up = (d_hidden * silu).astype(bf16)
    hidden_ref[...] = hidden
    d_gate_ref[...] = d_gate
    d_up_ref[...] = d_up
    final_ref[...] += dot(hidden, down, (1, 0))
    for spot, gate_part, up_part in parts:
        d_norm_ref[:, spot] += dot(d_gate, gate_part[...], (1, 1)) + dot(d_up, up_part[...], (1, 1))


def feed_forward(places, norm, dy, gates, ups, down):
    rows, width = norm.shape
    hidden_width = down.shape[0]
    block = 256
    still = lambda shape: pl.BlockSpec(shape, lambda j: (0, 0))
    along = lambda height: pl.BlockSpec((height, block), lambda j: (0, j))
    return pl.pallas_call(
        feed_kernel,
        grid=(hidden_width // block,),
        in_specs=[pl.BlockSpec(memory_space=pltpu.SMEM), still((rows, width)), still((rows, width))]
        + [along(part.shape[0]) for part in (*gates, *ups)]
        + [pl.BlockSpec((block, width), lambda j: (j, 0))],
        out_specs=[along(rows)] * 3 + [still((rows, width))] * 2,
        out_shape=[jax.ShapeDtypeStruct((rows, hidden_width), bf16)] * 3
        + [jax.ShapeDtypeStruct((rows, width), f32)] * 2,
        compiler_params=pltpu.CompilerParams(vmem_limit_bytes=36 * 1024 * 1024),
        cost_estimate=pl.CostEstimate(
            flops=12 * rows * width * hidden_width,
            bytes_accessed=6 * width * hidden_width,
            transcendentals=rows * hidden_width,
        ),
    )(places, norm, dy, *gates, *ups, down)


class Share:
    def __init__(self, links, partial, widths, halving, doubling):
        self.links, self.widths = links, widths
        groups, rows, self.cols = partial.shape
        self.rows = rows
        far = [("meet", (axis, axis)) for axis in range(3, links.bits)]
        self.steps = [("halve", axes) for axes in zip(*halving)] + far
        self.steps += [("double", axes) for axes in zip(*doubling)] + [("core", (0, 0))]
        self.left = (["fsdp", 1, 2], ["fsdp", 1, 2])
        self.data = partial.reshape((groups, 2, 2, 2, rows // 8, self.cols))
        self.outs = self.pending = None

    def cut(self, axes, other):
        links = self.links
        bits = [links.own(axis) for axis in axes]
        if other:
            bits = [1 - bit for bit in bits]
        dims = [1 + left.index(axis) for left, axis in zip(self.left, axes)]
        if dims[0] == dims[1]:
            return pick(self.data, bits[0] if axes[0] == axes[1] else links.by_core(bits), dims[0])
        return links.by_core([pick(self.data, bit, dim) for bit, dim in zip(bits, dims)])

    def receive(self, hold):
        if self.pending is None:
            return
        kind, axes, got = self.pending
        self.pending = None
        links, got = self.links, hold(got)
        if kind == "halve":
            kept = self.cut(axes, False)
            self.data = (kept.astype(f32) + got.astype(f32)).astype(bf16)
            for left, axis in zip(self.left, axes):
                left.remove(axis)
        elif kind == "meet":
            self.data = (self.data.astype(f32) + got.astype(f32)).astype(bf16)
        elif kind == "double":
            bits = [links.own(axis) for axis in axes]
            bit = bits[0] if axes[0] == axes[1] else links.by_core(bits)
            dims = [1 + sum(1 for o in left if o < axis) for left, axis in zip(self.left, axes)]
            data = in_order(bit, jnp.expand_dims(self.data, 1), jnp.expand_dims(got, 1), 1)
            moved = [jnp.moveaxis(data, 1, dim) for dim in dims]
            self.data = moved[0] if dims[0] == dims[1] else links.by_core(moved)
            for left, axis, dim in zip(self.left, axes, dims):
                left.insert(dim - 1, axis)
        else:
            shape = (self.data.shape[0], self.rows // 2, self.cols)
            own, other = self.data.reshape(shape), got.reshape(shape)
            self.outs = [
                out
                for i, widths in enumerate(self.widths)
                for out in finish_columns(self.links, own[i], other[i], widths)
            ]

    def step(self, after_last, hold):
        self.receive(after_last)
        kind, axes = self.steps.pop(0)
        send = self.cut(axes, True) if kind == "halve" else self.data
        got = self.links.swap_by_core(hold(send), axes)
        self.pending = (kind, axes, got)
        return got


def finish_kernel(widths, first_ref, own_ref, other_ref, *out_refs):
    first = first_ref[0] == 0
    low = jnp.where(first, own_ref[...], other_ref[...]).astype(f32)
    high = jnp.where(first, other_ref[...], own_ref[...]).astype(f32)
    offset = 0
    for width, out_ref in zip(widths, out_refs):
        half = width // 2
        out_ref[:, :half] = low[:, offset : offset + half]
        out_ref[:, half:] = high[:, offset : offset + half]
        offset += half


def finish_columns(links, own, other, widths):
    rows, cols = own.shape
    block = rows // 4
    spec = pl.BlockSpec((block, cols), lambda i: (i, 0))
    outs = pl.pallas_call(
        functools.partial(finish_kernel, widths),
        grid=(4,),
        in_specs=[pl.BlockSpec(memory_space=pltpu.SMEM), spec, spec],
        out_specs=[pl.BlockSpec((block, width), lambda i: (i, 0)) for width in widths],
        out_shape=[jax.ShapeDtypeStruct((rows, width), f32) for width in widths],
        compiler_params=pltpu.CompilerParams(vmem_limit_bytes=28 * 1024 * 1024),
        cost_estimate=pl.CostEstimate(flops=0, bytes_accessed=12 * own.size, transcendentals=0),
    )(links.own(0).reshape(1).astype(jnp.int32), own, other)
    return list(outs)


def half_columns(links, array, parts):
    mine = links.own(0)
    ours, theirs = [], []
    offset = 0
    for width in parts:
        piece = array[:, offset : offset + width]
        ours.append(lax.dynamic_slice_in_dim(piece, mine * (width // 2), width // 2, 1))
        theirs.append(lax.dynamic_slice_in_dim(piece, (1 - mine) * (width // 2), width // 2, 1))
        offset += width
    return join(ours), join(theirs)


def join(arrays):
    return arrays[0] if len(arrays) == 1 else jnp.concatenate(arrays, axis=1)


def with_other_core(links, ours, theirs):
    got = links.swap(join(theirs), 0)
    offset, outs = 0, []
    for array in ours:
        width = array.shape[1]
        outs.append(jnp.concatenate((array, got[:, offset : offset + width]), axis=0))
        offset += width
    return outs


def fence(*arrays):
    return lax.optimization_barrier(arrays)


def per_device(
    inputs,
    mixer_gain,
    query_weight,
    key_weight,
    value_weight,
    decay_down,
    decay_up,
    decay_bias,
    outgate_weight,
    head_gain,
    output_weight,
    feed_gain,
    feed_gate,
    feed_up,
    feed_down,
    cotangent,
):
    links = Links()
    seq_count, seg_rows, width = inputs.shape
    row_count = seq_count * seg_rows
    hidden_width = feed_gate.shape[1]
    key_cols, value_cols = H * DK, H * DV
    groups = links.seq_count // (seq_count * H)
    state_rows = DV // groups

    in_weights = (query_weight, key_weight, value_weight, outgate_weight)
    in_widths = (key_cols, key_cols, value_cols, value_cols)
    core = links.own(0)
    y_in = links.swap(join([own_piece(links, weight) for weight in in_weights]), "fsdp")
    piece_gate, piece_up = own_piece(links, feed_gate), core_half(links, feed_up)
    piece_out = jnp.concatenate(
        (own_piece(links, feed_down), own_piece(links, output_weight)), axis=0
    )
    out_rows = (feed_down.shape[0] // 4, output_weight.shape[0] // 4)
    full_in = lay_down(links, *in_weights)

    small = (mixer_gain, decay_down, decay_up, decay_bias, head_gain, feed_gain)
    packed = jnp.concatenate([piece.reshape(-1) for piece in small])
    packed_other = links.swap(packed, "fsdp")

    y_in = fence(y_in, full_in, piece_out, piece_gate, piece_up)[0]
    x_in = links.swap_by_core(y_in, near_bits)
    y_out = links.swap(fence(piece_out, y_in)[0], "fsdp")
    near_in = near_half(links, y_in, x_in)
    far_in = links.swap(near_in, 0)
    full_in = fill_other(links, full_in, near_in, far_in)

    low_half = jnp.where(links.fsdp == 0, packed, packed_other)
    high_half = jnp.where(links.fsdp == 0, packed_other, packed)
    whole_small = []
    offset = 0
    for piece in small:
        parts = [half[offset : offset + piece.size].reshape(piece.shape) for half in (low_half, high_half)]
        whole_small.append(jnp.concatenate(parts, axis=0))
        offset += piece.size
    full_mixer_gain, full_down, full_up_rank, full_bias, full_head_gain, full_feed_gain = whole_small
    head_gain_row = full_head_gain.astype(f32).reshape(1, DV)

    residual_in = inputs.reshape(row_count, width).astype(f32)
    normed_full, first_pull = jax.vjp(rms_scale, residual_in, full_mixer_gain.astype(f32))
    normed = normed_full.astype(bf16)
    projected = mat_product(normed, full_in)
    query = projected[:, :key_cols].astype(bf16)
    keys = projected[:, key_cols : 2 * key_cols].astype(bf16)
    values = projected[:, 2 * key_cols : 2 * key_cols + value_cols].astype(bf16)
    out_gate = projected[:, 2 * key_cols + value_cols :]
    ranked = mat_product(normed, full_down).astype(bf16)
    decay_in = mat_product(ranked, full_up_rank) + full_bias.astype(f32)
    decay = (jax.nn.log_sigmoid(decay_in) / gate_scale).astype(bf16)

    qkg_specs = [row_spec(key_cols)] * 3
    rows_wide = row_spec(value_cols)
    gain_spec = pl.BlockSpec((1, DV), lambda i: (0, 0))
    whole_state = pl.BlockSpec((H, DV, DK), lambda i: (i, 0, 0))
    wide_shape = jax.ShapeDtypeStruct((row_count, value_cols), bf16)
    block_flops = 2 * SPAN * DK * DV * 6

    def to_heads(array):
        rows = array.shape[2]
        return lax.all_to_all(
            array.reshape(links.seq_count, rows, DK), "seq", split_axis=0, concat_axis=0, tiled=True
        )

    def to_tokens(array):
        back = lax.all_to_all(array, "seq", split_axis=0, concat_axis=0, tiled=True)
        return back.reshape(seq_count * H, DV, DK)

    inside, update = block_call(
        local_kernel,
        seq_count,
        qkg_specs + [rows_wide],
        [rows_wide, state_spec(groups, state_rows + 16)],
        [
            jax.ShapeDtypeStruct((row_count, value_cols), f32),
            jax.ShapeDtypeStruct((seq_count * H, groups, state_rows + 16, DK), bf16),
        ],
        2 * block_flops,
    )(query, keys, decay, values)
    y_gate = links.swap(fence(piece_gate, y_out, update)[0], "fsdp")
    near_up = links.swap(fence(piece_up, y_gate)[0], "fsdp")
    y_out = fence(y_out, update)[0]
    x_out = links.swap_by_core(y_out, near_bits)
    x_gate = links.swap_by_core(y_gate, near_bits)
    received = to_heads(update)
    before = scan_blocks(False, received, received)
    near_up, x_gate = fence(near_up, before)[0], fence(x_gate, before)[0]
    full_feed_down = lay_down(links, fence(feed_down, update)[0])
    full_output = lay_down(links, fence(output_weight, update)[0])
    near_down = near_half(links, y_out[: out_rows[0]], x_out[: out_rows[0]])
    near_output = near_half(links, y_out[out_rows[0] :], x_out[out_rows[0] :])
    far_out = links.swap(jnp.concatenate((near_down, near_output), axis=0), 0)
    far_down, far_output = far_out[: 2 * out_rows[0]], far_out[2 * out_rows[0] :]
    full_feed_down = fill_other(links, full_feed_down, near_down, far_down)
    full_output = fill_other(links, full_output, near_output, far_output)
    near_gate = near_half(links, y_gate, x_gate)
    far_gate = links.swap(near_gate, 0)
    far_up = links.swap(near_up, 0)
    d_down = cotangent.reshape(row_count, width)
    seq_grad = d_down.astype(f32)
    down_ours, down_theirs = half_columns(links, d_down, (width,))
    normed_both, down_both = with_other_core(
        links, (normed, down_ours), (fence(normed, update)[0], down_theirs)
    )
    state = to_tokens(before)
    mixed, gated = block_call(
        outside_kernel,
        seq_count,
        qkg_specs + [rows_wide, whole_state, rows_wide, gain_spec],
        [rows_wide] * 2,
        [wide_shape] * 2,
        block_flops,
    )(query, keys, decay, inside, state, out_gate, head_gain_row)


    gated = fence(gated, normed_both, down_both)[0]
    middle = residual_in + mat_product(gated, full_output)
    second_full, second_pull = jax.vjp(rms_scale, middle, full_feed_gain.astype(f32))
    second_norm = second_full.astype(bf16)
    half = width // 2
    other_base = (1 - links.fsdp) * half
    places = jnp.stack(
        (links.fsdp * half, other_base + core * (half // 2), other_base + (1 - core) * (half // 2))
    ).astype(jnp.int32)
    hidden, d_gate, d_up, fed, d_second = feed_forward(
        places,
        second_norm,
        d_down,
        (feed_gate, near_gate, far_gate),
        (feed_up, near_up, far_up),
        full_feed_down,
    )
    output = (middle + fed).astype(bf16).reshape(seq_count, seg_rows, width)

    (second_both,) = with_other_core(links, (second_norm,), (second_norm,))
    (hidden_both,) = with_other_core(links, (hidden,), (hidden,))
    grad_down = cross_rows(hidden_both, down_both).astype(bf16)

    x, y, z = 1, "fsdp", 2
    cuts = (([y, x, z], [x, z, y]), ([y, z, x], [z, x, y]), ([y, x, z], [y, z, x]))
    joins = ([z, x], [x, z])
    shares, arrived, sent, extras = {}, [], [], []

    def after_last(array):
        return fence(array, *sent[-1:])[0]

    def hold(array, *due):
        behind = (*arrived[-4:-3], *sent[-1:], *extras, *due)
        sent.append(array)
        return fence(array, *behind)[0]

    def go(*names):
        for name in names:
            share = shares[name]
            if not share.steps:
                share.receive(after_last)
                sent.append(share.outs[0])
                continue
            arrived.append(share.step(after_last, hold))
            while share.steps and share.steps[0][0] == "meet" and share.steps[0][1][0] > 3:
                arrived.append(share.step(after_last, hold))

    shares["down"] = Share(links, grad_down[None], [(width,)], cuts[0], joins)
    go("down")
    d_second = fence(d_second, sent[0])[0]

    gate_ours, gate_theirs = half_columns(links, d_gate, (hidden_width,))
    up_ours, up_theirs = half_columns(links, d_up, (hidden_width,))
    gate_both, up_both = with_other_core(links, (gate_ours, up_ours), (gate_theirs, up_theirs))
    grad_gate = cross_rows(second_both, gate_both).astype(bf16)
    grad_up = cross_rows(second_both, up_both).astype(bf16)

    d_middle_norm, grad_feed_gain = second_pull(d_second)
    d_middle = seq_grad + d_middle_norm
    d_branch = d_middle.astype(bf16)
    d_gated = back_product(d_branch, full_output)
    d_mixed, d_outgate, gain_parts, back_update = block_call(
        back_state_kernel,
        seq_count,
        qkg_specs + [rows_wide] * 3 + [gain_spec],
        [rows_wide] * 2
        + [pl.BlockSpec((1, 8, DV), lambda i: (i, 0, 0)), state_spec(groups, state_rows)],
        [wide_shape] * 2
        + [
            jax.ShapeDtypeStruct((seq_count, 8, DV), f32),
            jax.ShapeDtypeStruct((seq_count * H, groups, state_rows, DK), bf16),
        ],
        block_flops,
    )(query, keys, decay, d_gated, mixed, out_gate, head_gain_row)
    grad_head_gain = jnp.sum(gain_parts, axis=(0, 1))
    branch_ours, branch_theirs = half_columns(links, d_branch, (width,))
    outgate_ours, outgate_theirs = half_columns(links, d_outgate, (value_cols,))
    gated_both, branch_both, outgate_both = with_other_core(
        links, (gated, branch_ours, outgate_ours), (gated, branch_theirs, outgate_theirs)
    )
    grad_mixer_out = fence(
        jnp.stack(
            (
                cross_rows(gated_both, branch_both).astype(bf16),
                cross_rows(normed_both, outgate_both).astype(bf16),
            )
        )
    )[0]

    back_received = to_heads(hold(back_update))
    shares["gate"] = Share(links, grad_gate[None], [(hidden_width,)], cuts[1], joins)
    shares["out"] = Share(links, grad_mixer_out, [(width,), (value_cols,)], cuts[0], joins)
    shares["up"] = Share(links, grad_up[None], [(hidden_width,)], cuts[2], joins)
    go("gate", "out", "down")
    after = to_tokens(hold(scan_blocks(True, received, after_last(back_received))))
    go("up", "gate", "down")
    after = after_last(after)
    d_query, d_keys, d_decay, d_values = block_call(
        back_kernel,
        seq_count,
        qkg_specs + [rows_wide] * 2 + [whole_state] * 2,
        [row_spec(key_cols)] * 3 + [rows_wide],
        [jax.ShapeDtypeStruct((row_count, key_cols), bf16)] * 3 + [wide_shape],
        4 * block_flops,
    )(query, keys, decay, values, d_mixed, state, after)
    d_qkv = jnp.concatenate((d_query, d_keys, d_values), axis=1)
    qkv_ours, qkv_theirs = half_columns(links, d_qkv, in_widths[:3])
    (qkv_both,) = with_other_core(links, (qkv_ours,), (qkv_theirs,))
    grad_qkv = cross_rows(normed_both, qkv_both).astype(bf16)
    shares["qkv"] = Share(links, grad_qkv[None], [in_widths[:3]], cuts[1], joins)
    sent.append(d_query)
    go("qkv")
    d_qkv, d_decay, _ = fence(d_qkv, d_decay, sent[-1])

    d_decay_in = d_decay.astype(f32) * jax.nn.sigmoid(-decay_in) / gate_scale
    grad_decay_bias = jnp.sum(d_decay_in, axis=0)
    grad_decay_up = lax.dot_general(
        ranked.astype(f32), d_decay_in, (((0,), (0,)), ((), ())), precision=highest
    )
    d_ranked = lax.dot_general(
        d_decay_in, full_up_rank.astype(f32), (((1,), (1,)), ((), ())), precision=highest
    ).astype(bf16)
    grad_decay_down = cross_rows(normed, d_ranked)
    d_normed = back_product(
        jnp.concatenate((d_qkv, d_outgate), axis=1), full_in
    ) + back_product(d_ranked, full_down)
    d_input_norm, grad_mixer_gain = first_pull(d_normed)
    input_grad = (d_middle + d_input_norm).reshape(seq_count, seg_rows, width)

    small_grads = (
        grad_mixer_gain, grad_decay_down, grad_decay_up, grad_decay_bias, grad_head_gain,
        grad_feed_gain,
    )
    total = jnp.concatenate([grad.reshape(2, -1) for grad in small_grads], axis=1)
    go("up", "gate", "down", "out")
    other = links.swap(hold(pick(total, 1 - links.fsdp), input_grad, output), "fsdp")
    go("up", "qkv", "gate")
    total = (pick(total, links.fsdp) + after_last(other)).reshape(links.seq_count, -1)
    pieces = lax.all_to_all(hold(total), "seq", split_axis=0, concat_axis=0, tiled=True)
    go("out", "qkv", "up", "gate")
    own_sum = jnp.sum(after_last(pieces), axis=0, keepdims=True)
    own_sum = hold(jnp.broadcast_to(own_sum, total.shape))
    total = lax.all_to_all(own_sum, "seq", split_axis=0, concat_axis=0, tiled=True)
    go("down", "out", "up", "down", "qkv", "gate")
    total = after_last(total).reshape(-1)
    small_out = []
    offset = 0
    for grad in small_grads:
        size = grad.size // 2
        small_out.append(
            total[offset : offset + size].reshape((grad.shape[0] // 2,) + grad.shape[1:])
        )
        offset += size
    out_mixer_gain, out_decay_down, out_decay_up, out_bias, out_head_gain, out_feed_gain = small_out
    extras.extend(small_out)
    go("qkv", "out", "up", "down", "qkv", "down", "out", "gate", "qkv", "up", "gate", "out", "qkv", "up", "out")
    results = [
        out for name in ("down", "gate", "up", "out", "qkv") for out in shares[name].outs
    ]


    (
        out_down, out_gate_w, out_up_w, out_output, out_outgate, out_query, out_key, out_value,
    ) = results
    return (
        output,
        input_grad,
        out_mixer_gain,
        out_query,
        out_key,
        out_value,
        out_decay_down,
        out_decay_up,
        out_bias,
        out_outgate,
        out_head_gain,
        out_output,
        out_feed_gain,
        out_gate_w,
        out_up_w,
        out_down,
    )


def solution(mesh):
    rows = P("fsdp", None)
    gains = P("fsdp")
    tokens = P("fsdp", "seq", None)
    weights = (gains, rows, rows, rows, rows, rows, gains, rows, gains, rows, gains, rows, rows, rows)
    return jax.shard_map(
        per_device,
        mesh=mesh,
        in_specs=(tokens,) + weights + (tokens,),
        out_specs=(tokens, tokens) + weights,
        check_vma=False,
    )
```

```python
import functools

import jax
import jax.numpy as jnp
from jax import lax
from jax.experimental import pallas as pl
from jax.experimental.pallas import tpu as pltpu
from jax.sharding import PartitionSpec as P

H = 4
DK = 128
DV = 256
SPAN = 64


epsilon = 1e-06
head_floor = 0.25
gate_scale = 16.0
highest = lax.Precision.HIGHEST
bf16 = jnp.bfloat16
f32 = jnp.float32


def rms_scale(values, scale_gain):
    return (
        values * lax.rsqrt(jnp.mean(values * values, axis=-1, keepdims=True) + epsilon) * scale_gain
    )


def mat_product(left, right):
    return jnp.dot(left, right, preferred_element_type=f32)


def cross_rows(left, right):
    return lax.dot_general(left, right, (((0,), (0,)), ((), ())), preferred_element_type=f32)


def back_product(left, right):
    return lax.dot_general(left, right, (((1,), (1,)), ((), ())), preferred_element_type=f32)


def dot(left, right, contract):
    return lax.dot_general(
        left, right, (((contract[0],), (contract[1],)), ((), ())), preferred_element_type=f32
    )


def fine(left, right, contract):
    lefts, rights = parts_of(left), parts_of(right)
    total = dot(lefts[0], rights[0], contract)
    if len(lefts) > 1:
        total = total + dot(lefts[1], rights[0], contract)
    if len(rights) > 1:
        total = total + dot(lefts[0], rights[1], contract)
    return total


def parts_of(array):
    if array.dtype == bf16:
        return (array,)
    high = array.astype(bf16)
    return high, (array - high.astype(f32)).astype(bf16)


def triangle():
    rows = lax.broadcasted_iota(jnp.int32, (SPAN, SPAN), 0)
    cols = lax.broadcasted_iota(jnp.int32, (SPAN, SPAN), 1)
    return rows >= cols


def block_terms(q_ref, k_ref, g_ref, head):
    cols = slice(head * DK, (head + 1) * DK)
    lower = jnp.where(triangle(), 1.0, 0.0).astype(bf16)
    c = jnp.dot(lower, g_ref[:, cols], preferred_element_type=f32)
    e = c[SPAN - 1 : SPAN, :]
    qt = q_ref[:, cols].astype(f32) * DK ** (-0.5) * jnp.exp(c)
    keys = k_ref[:, cols].astype(f32)
    return c, e, qt, keys * jnp.exp(-c), keys * jnp.exp(e - c)


def store_groups(ref, head, state):
    groups, size = ref.shape[1], ref.shape[2]
    count = state.shape[0] // groups
    for group in range(groups):
        ref[head, group, 0:count, :] = state[group * count : (group + 1) * count, :].astype(bf16)


def local_kernel(q_ref, k_ref, g_ref, v_ref, inside_ref, send_ref):
    groups = send_ref.shape[1]
    count = DV // groups
    place = lax.broadcasted_iota(jnp.int32, (16, DK), 0)
    for head in range(H):
        wide = slice(head * DV, (head + 1) * DV)
        c, e, qt, kt, kl = block_terms(q_ref, k_ref, g_ref, head)
        v = v_ref[:, wide]
        scores = jnp.where(triangle(), fine(qt, kt, (1, 1)), 0.0)
        inside_ref[:, wide] = fine(scores, v, (1, 0))
        store_groups(send_ref, head, fine(v, kl, (0, 0)))
        fade = jnp.exp(e)
        high = fade.astype(bf16).astype(f32)
        tail = jnp.where(place == 0, high, jnp.where(place == 1, fade - high, 0.0)).astype(bf16)
        for group in range(groups):
            send_ref[head, group, count : count + 16, :] = tail


def scan_kernel(backward, fade_ref, update_ref, before_ref):
    blocks, count, _ = before_ref.shape

    def step(i, state):
        block = blocks - 1 - i if backward else i
        before_ref[block] = state.astype(bf16)
        tail = fade_ref[block, count : count + 16, :].astype(f32)
        fade = tail[0:1, :] + tail[1:2, :]
        return state * fade + update_ref[block, 0:count, :].astype(f32)

    lax.fori_loop(0, blocks, step, jnp.zeros((count, DK), f32), unroll=4)


def scan_blocks(backward, received_fade, received):
    blocks, rows, _ = received_fade.shape
    return pl.pallas_call(
        functools.partial(scan_kernel, backward),
        out_shape=jax.ShapeDtypeStruct((blocks, rows - 16, DK), bf16),
        in_specs=[pl.BlockSpec(memory_space=pltpu.VMEM)] * 2,
        out_specs=pl.BlockSpec(memory_space=pltpu.VMEM),
        compiler_params=pltpu.CompilerParams(vmem_limit_bytes=24 * 1024 * 1024),
        cost_estimate=pl.CostEstimate(
            flops=4 * received.size, bytes_accessed=6 * received.size, transcendentals=0
        ),
    )(received_fade, received)


def outside_kernel(q_ref, k_ref, g_ref, inside_ref, state_ref, gate_ref, gain_ref, mixed_ref, gated_ref):
    for head in range(H):
        wide = slice(head * DV, (head + 1) * DV)
        c, e, qt, kt, kl = block_terms(q_ref, k_ref, g_ref, head)
        mixed = (inside_ref[:, wide] + fine(qt, state_ref[head], (1, 1))).astype(bf16)
        mixed_ref[:, wide] = mixed
        m = mixed.astype(f32)
        gate = gate_ref[:, wide]
        scale = lax.rsqrt(jnp.maximum(jnp.mean(m * m, axis=1, keepdims=True), head_floor))
        gated_ref[:, wide] = (m * scale * gain_ref[...] * (gate * jax.nn.sigmoid(gate))).astype(bf16)


def back_state_kernel(
    q_ref, k_ref, g_ref, dy_ref, mixed_ref, gate_ref, gain_ref,
    d_mixed_ref, d_gate_ref, gain_grad_ref, send_ref,
):
    gain_grad = jnp.zeros((1, DV), f32)
    gain = gain_ref[...]
    for head in range(H):
        wide = slice(head * DV, (head + 1) * DV)
        c, e, qt, kt, kl = block_terms(q_ref, k_ref, g_ref, head)
        m = mixed_ref[:, wide].astype(f32)
        gate = gate_ref[:, wide]
        dy = dy_ref[:, wide]
        square = jnp.mean(m * m, axis=1, keepdims=True)
        scale = lax.rsqrt(jnp.maximum(square, head_floor))
        sig = jax.nn.sigmoid(gate)
        silu = gate * sig
        unit = m * scale
        d_gate_ref[:, wide] = (dy * unit * gain * (sig * (1.0 + gate * (1.0 - sig)))).astype(bf16)
        d_normed = dy * silu
        gain_grad = gain_grad + jnp.sum(d_normed * unit, axis=0, keepdims=True)
        t = d_normed * gain
        inner = jnp.sum(t * m, axis=1, keepdims=True) * (1.0 / DV)
        share = jnp.where(square > head_floor, 1.0, jnp.where(square == head_floor, 0.5, 0.0))
        d_mixed = (t * scale - m * (inner * share * scale * scale * scale)).astype(bf16)
        d_mixed_ref[:, wide] = d_mixed
        store_groups(send_ref, head, fine(d_mixed, qt, (0, 0)))
    gain_grad_ref[0] = jnp.broadcast_to(gain_grad, (8, DV)) * 0.125


def back_kernel(
    q_ref, k_ref, g_ref, v_ref, do_ref, state_ref, after_ref, dq_ref, dk_ref, dg_ref, dv_ref
):
    mask = triangle()
    upper = jnp.where(
        lax.broadcasted_iota(jnp.int32, (SPAN, SPAN), 0)
        <= lax.broadcasted_iota(jnp.int32, (SPAN, SPAN), 1),
        1.0,
        0.0,
    ).astype(bf16)
    last = lax.broadcasted_iota(jnp.int32, (SPAN, DK), 0) == SPAN - 1
    for head in range(H):
        wide = slice(head * DV, (head + 1) * DV)
        cols = slice(head * DK, (head + 1) * DK)
        c, e, qt, kt, kl = block_terms(q_ref, k_ref, g_ref, head)
        v = v_ref[:, wide]
        do = do_ref[:, wide]
        state = state_ref[head]
        after = after_ref[head]
        scores = jnp.where(mask, fine(qt, kt, (1, 1)), 0.0)
        d_scores = jnp.where(mask, fine(do, v, (1, 1)), 0.0)
        dv_ref[:, wide] = (fine(scores, do, (0, 0)) + fine(kl, after, (1, 1))).astype(bf16)
        dqt = fine(d_scores, kt, (1, 0)) + fine(do, state, (1, 0))
        dkt = fine(d_scores, qt, (0, 0))
        dkl = fine(v, after, (1, 0))
        dq_ref[:, cols] = (dqt * (DK ** (-0.5) * jnp.exp(c))).astype(bf16)
        dk_ref[:, cols] = (dkt * jnp.exp(-c) + dkl * jnp.exp(e - c)).astype(bf16)
        tail = kl * dkl
        fade_grad = jnp.sum(after.astype(f32) * state.astype(f32), axis=0, keepdims=True)
        de = jnp.sum(tail, axis=0, keepdims=True) + jnp.exp(e) * fade_grad
        dc = qt * dqt - kt * dkt - tail + jnp.where(last, de, 0.0)
        dg_ref[:, cols] = fine(upper, dc, (1, 0)).astype(bf16)


def row_spec(width):
    return pl.BlockSpec((SPAN, width), lambda i: (i, 0))


def state_spec(groups, count):
    return pl.BlockSpec((H, groups, count, DK), lambda i: (i, 0, 0, 0))


def block_call(kernel, seq_count, in_specs, out_specs, out_shape, flops):
    return pl.pallas_call(
        kernel,
        grid=(seq_count,),
        in_specs=in_specs,
        out_specs=out_specs,
        out_shape=out_shape,
        compiler_params=pltpu.CompilerParams(vmem_limit_bytes=24 * 1024 * 1024),
        cost_estimate=pl.CostEstimate(
            flops=flops * seq_count * H, bytes_accessed=4 * 1024 * 1024, transcendentals=0
        ),
    )


class Links:
    def __init__(self):
        self.fsdp = lax.axis_index("fsdp")
        self.seq = lax.axis_index("seq")
        self.seq_count = lax.axis_size("seq")
        self.bits = self.seq_count.bit_length() - 1

    def own(self, axis):
        return self.fsdp if axis == "fsdp" else lax.rem(lax.div(self.seq, 1 << axis), 2)

    def swap_by_core(self, array, axes):
        if axes[0] == axes[1]:
            return self.swap(array, axes[0])
        count, moves = self.seq_count, []
        for fsdp in range(2):
            for seq in range(count):
                axis = axes[seq % 2]
                to = (1 - fsdp, seq) if axis == "fsdp" else (fsdp, seq ^ (1 << axis))
                moves.append((fsdp * count + seq, to[0] * count + to[1]))
        return lax.ppermute(array, ("fsdp", "seq"), moves)

    def by_core(self, pair):
        return jnp.where(self.own(0) == 0, pair[0], pair[1])

    def swap(self, array, axis):
        if axis == "fsdp":
            return lax.ppermute(array, "fsdp", [(0, 1), (1, 0)])
        return lax.ppermute(
            array, "seq", [(i, i ^ (1 << axis)) for i in range(self.seq_count)]
        )


def pick(array, index, axis=0):
    return lax.dynamic_index_in_dim(array, index, axis, keepdims=False)


def in_order(bit, own, other, axis):
    size = own.shape[axis]
    shape = list(own.shape)
    shape[axis] = 2 * size
    whole = jnp.zeros(shape, own.dtype)
    whole = lax.dynamic_update_slice_in_dim(whole, own, bit * size, axis)
    return lax.dynamic_update_slice_in_dim(whole, other, (1 - bit) * size, axis)


def own_piece(links, array):
    rows = array.shape[0] // 4
    bit = links.by_core([links.own(axis) for axis in near_bits])
    return lax.dynamic_slice_in_dim(array, (links.own(0) * 2 + bit) * rows, rows, 0)


near_bits = (1, 2)


def near_half(links, own, other):
    return in_order(links.by_core([links.own(axis) for axis in near_bits]), own, other, 0)


def core_half(links, array):
    rows = array.shape[0] // 2
    return lax.dynamic_slice_in_dim(array, links.own(0) * rows, rows, 0)


def lay_down(links, *arrays):
    rows = arrays[0].shape[0]
    whole = jnp.zeros((2 * rows, sum(array.shape[1] for array in arrays)), bf16)
    col = 0
    for array in arrays:
        whole = lax.dynamic_update_slice(whole, array, (links.fsdp * rows, col))
        col += array.shape[1]
    return whole


def fill_other(links, whole, near, far):
    rows = whole.shape[0] // 2
    base = (1 - links.fsdp) * rows
    core = links.own(0)
    whole = lax.dynamic_update_slice(whole, near, (base + core * (rows // 2), 0))
    return lax.dynamic_update_slice(whole, far, (base + (1 - core) * (rows // 2), 0))


def feed_kernel(
    place_ref, norm_ref, dy_ref, gate_own, gate_near, gate_far, up_own, up_near, up_far, down_ref,
    hidden_ref, d_gate_ref, d_up_ref, final_ref, d_norm_ref,
):
    @pl.when(pl.program_id(0) == 0)
    def _():
        final_ref[...] = jnp.zeros_like(final_ref)
        d_norm_ref[...] = jnp.zeros_like(d_norm_ref)

    parts = []
    for i, (gate_part, up_part) in enumerate(
        ((gate_own, up_own), (gate_near, up_near), (gate_far, up_far))
    ):
        rows = gate_part.shape[0]
        parts.append((pl.ds(pl.multiple_of(place_ref[i], rows), rows), gate_part, up_part))
    gate = sum(dot(norm_ref[:, spot], part[...], (1, 0)) for spot, part, _ in parts)
    up = sum(dot(norm_ref[:, spot], part[...], (1, 0)) for spot, _, part in parts)
    down = down_ref[...]
    d_hidden = dot(dy_ref[...], down, (1, 1))
    sig = jax.nn.sigmoid(gate)
    silu = gate * sig
    hidden = (silu * up).astype(bf16)
    d_gate = (d_hidden * up * (sig * (1.0 + gate * (1.0 - sig)))).astype(bf16)
    d_up = (d_hidden * silu).astype(bf16)
    hidden_ref[...] = hidden
    d_gate_ref[...] = d_gate
    d_up_ref[...] = d_up
    final_ref[...] += dot(hidden, down, (1, 0))
    for spot, gate_part, up_part in parts:
        d_norm_ref[:, spot] += dot(d_gate, gate_part[...], (1, 1)) + dot(d_up, up_part[...], (1, 1))


def feed_forward(places, norm, dy, gates, ups, down):
    rows, width = norm.shape
    hidden_width = down.shape[0]
    block = 256
    still = lambda shape: pl.BlockSpec(shape, lambda j: (0, 0))
    along = lambda height: pl.BlockSpec((height, block), lambda j: (0, j))
    return pl.pallas_call(
        feed_kernel,
        grid=(hidden_width // block,),
        in_specs=[pl.BlockSpec(memory_space=pltpu.SMEM), still((rows, width)), still((rows, width))]
        + [along(part.shape[0]) for part in (*gates, *ups)]
        + [pl.BlockSpec((block, width), lambda j: (j, 0))],
        out_specs=[along(rows)] * 3 + [still((rows, width))] * 2,
        out_shape=[jax.ShapeDtypeStruct((rows, hidden_width), bf16)] * 3
        + [jax.ShapeDtypeStruct((rows, width), f32)] * 2,
        compiler_params=pltpu.CompilerParams(vmem_limit_bytes=36 * 1024 * 1024),
        cost_estimate=pl.CostEstimate(
            flops=12 * rows * width * hidden_width,
            bytes_accessed=6 * width * hidden_width,
            transcendentals=rows * hidden_width,
        ),
    )(places, norm, dy, *gates, *ups, down)


class Share:
    def __init__(self, links, partial, widths, halving, doubling):
        self.links, self.widths = links, widths
        groups, rows, self.cols = partial.shape
        self.rows = rows
        far = [("meet", (axis, axis)) for axis in range(3, links.bits)]
        self.steps = [("halve", axes) for axes in zip(*halving)] + far
        self.steps += [("double", axes) for axes in zip(*doubling)] + [("core", (0, 0))]
        self.left = (["fsdp", 1, 2], ["fsdp", 1, 2])
        self.data = partial.reshape((groups, 2, 2, 2, rows // 8, self.cols))
        self.outs = self.pending = None

    def cut(self, axes, other):
        links = self.links
        bits = [links.own(axis) for axis in axes]
        if other:
            bits = [1 - bit for bit in bits]
        dims = [1 + left.index(axis) for left, axis in zip(self.left, axes)]
        if dims[0] == dims[1]:
            return pick(self.data, bits[0] if axes[0] == axes[1] else links.by_core(bits), dims[0])
        return links.by_core([pick(self.data, bit, dim) for bit, dim in zip(bits, dims)])

    def receive(self, hold):
        if self.pending is None:
            return
        kind, axes, got = self.pending
        self.pending = None
        links, got = self.links, hold(got)
        if kind == "halve":
            kept = self.cut(axes, False)
            self.data = (kept.astype(f32) + got.astype(f32)).astype(bf16)
            for left, axis in zip(self.left, axes):
                left.remove(axis)
        elif kind == "meet":
            self.data = (self.data.astype(f32) + got.astype(f32)).astype(bf16)
        elif kind == "double":
            bits = [links.own(axis) for axis in axes]
            bit = bits[0] if axes[0] == axes[1] else links.by_core(bits)
            dims = [1 + sum(1 for o in left if o < axis) for left, axis in zip(self.left, axes)]
            data = in_order(bit, jnp.expand_dims(self.data, 1), jnp.expand_dims(got, 1), 1)
            moved = [jnp.moveaxis(data, 1, dim) for dim in dims]
            self.data = moved[0] if dims[0] == dims[1] else links.by_core(moved)
            for left, axis, dim in zip(self.left, axes, dims):
                left.insert(dim - 1, axis)
        else:
            shape = (self.data.shape[0], self.rows // 2, self.cols)
            own, other = self.data.reshape(shape), got.reshape(shape)
            self.outs = finish_columns(self.links, own, other, self.widths)

    def step(self, after_last, hold):
        self.receive(after_last)
        kind, axes = self.steps.pop(0)
        send = self.cut(axes, True) if kind == "halve" else self.data
        got = self.links.swap_by_core(hold(send), axes)
        self.pending = (kind, axes, got)
        return got


def finish_kernel(widths, first_ref, own_ref, other_ref, *out_refs):
    first = first_ref[0] == 0
    targets = list(out_refs)
    for group, group_widths in enumerate(widths):
        own, other = own_ref[group], other_ref[group]
        low = jnp.where(first, own, other).astype(f32)
        high = jnp.where(first, other, own).astype(f32)
        offset = 0
        for width in group_widths:
            half, out_ref = width // 2, targets.pop(0)
            out_ref[:, :half] = low[:, offset : offset + half]
            out_ref[:, half:] = high[:, offset : offset + half]
            offset += half


def finish_columns(links, own, other, widths):
    groups, rows, cols = own.shape
    block = rows // 4
    spec = pl.BlockSpec((groups, block, cols), lambda i: (0, i, 0))
    flat = [width for group_widths in widths for width in group_widths]
    outs = pl.pallas_call(
        functools.partial(finish_kernel, widths),
        grid=(4,),
        in_specs=[pl.BlockSpec(memory_space=pltpu.SMEM), spec, spec],
        out_specs=[pl.BlockSpec((block, width), lambda i: (i, 0)) for width in flat],
        out_shape=[jax.ShapeDtypeStruct((rows, width), f32) for width in flat],
        compiler_params=pltpu.CompilerParams(vmem_limit_bytes=28 * 1024 * 1024),
        cost_estimate=pl.CostEstimate(flops=0, bytes_accessed=12 * own.size, transcendentals=0),
    )(links.own(0).reshape(1).astype(jnp.int32), own, other)
    return list(outs)


def half_columns(links, array, parts):
    mine = links.own(0)
    ours, theirs = [], []
    offset = 0
    for width in parts:
        piece = array[:, offset : offset + width]
        ours.append(lax.dynamic_slice_in_dim(piece, mine * (width // 2), width // 2, 1))
        theirs.append(lax.dynamic_slice_in_dim(piece, (1 - mine) * (width // 2), width // 2, 1))
        offset += width
    return join(ours), join(theirs)


def join(arrays):
    return arrays[0] if len(arrays) == 1 else jnp.concatenate(arrays, axis=1)


def with_other_core(links, ours, theirs):
    got = links.swap(join(theirs), 0)
    offset, outs = 0, []
    for array in ours:
        width = array.shape[1]
        outs.append(jnp.concatenate((array, got[:, offset : offset + width]), axis=0))
        offset += width
    return outs


def fence(*arrays):
    return lax.optimization_barrier(arrays)


def per_device(
    inputs,
    mixer_gain,
    query_weight,
    key_weight,
    value_weight,
    decay_down,
    decay_up,
    decay_bias,
    outgate_weight,
    head_gain,
    output_weight,
    feed_gain,
    feed_gate,
    feed_up,
    feed_down,
    cotangent,
):
    links = Links()
    seq_count, seg_rows, width = inputs.shape
    row_count = seq_count * seg_rows
    hidden_width = feed_gate.shape[1]
    key_cols, value_cols = H * DK, H * DV
    groups = links.seq_count // (seq_count * H)
    state_rows = DV // groups

    in_weights = (query_weight, key_weight, value_weight, outgate_weight)
    in_widths = (key_cols, key_cols, value_cols, value_cols)
    core = links.own(0)
    y_in = links.swap(join([own_piece(links, weight) for weight in in_weights]), "fsdp")
    piece_gate, piece_up = own_piece(links, feed_gate), core_half(links, feed_up)
    piece_out = jnp.concatenate(
        (own_piece(links, feed_down), own_piece(links, output_weight)), axis=0
    )
    out_rows = (feed_down.shape[0] // 4, output_weight.shape[0] // 4)
    full_in = lay_down(links, *in_weights)

    small = (mixer_gain, decay_down, decay_up, decay_bias, head_gain, feed_gain)
    packed = jnp.concatenate([piece.reshape(-1) for piece in small])
    packed_other = links.swap(packed, "fsdp")

    y_in = fence(y_in, full_in, piece_out, piece_gate, piece_up)[0]
    x_in = links.swap_by_core(y_in, near_bits)
    y_out = links.swap(fence(piece_out, y_in)[0], "fsdp")
    near_in = near_half(links, y_in, x_in)
    far_in = links.swap(near_in, 0)
    full_in = fill_other(links, full_in, near_in, far_in)

    low_half = jnp.where(links.fsdp == 0, packed, packed_other)
    high_half = jnp.where(links.fsdp == 0, packed_other, packed)
    whole_small = []
    offset = 0
    for piece in small:
        parts = [half[offset : offset + piece.size].reshape(piece.shape) for half in (low_half, high_half)]
        whole_small.append(jnp.concatenate(parts, axis=0))
        offset += piece.size
    full_mixer_gain, full_down, full_up_rank, full_bias, full_head_gain, full_feed_gain = whole_small
    head_gain_row = full_head_gain.astype(f32).reshape(1, DV)

    residual_in = inputs.reshape(row_count, width).astype(f32)
    normed_full, first_pull = jax.vjp(rms_scale, residual_in, full_mixer_gain.astype(f32))
    normed = normed_full.astype(bf16)
    projected = mat_product(normed, full_in)
    query = projected[:, :key_cols].astype(bf16)
    keys = projected[:, key_cols : 2 * key_cols].astype(bf16)
    values = projected[:, 2 * key_cols : 2 * key_cols + value_cols].astype(bf16)
    out_gate = projected[:, 2 * key_cols + value_cols :]
    ranked = mat_product(normed, full_down).astype(bf16)
    decay_in = mat_product(ranked, full_up_rank) + full_bias.astype(f32)
    decay = (jax.nn.log_sigmoid(decay_in) / gate_scale).astype(bf16)

    qkg_specs = [row_spec(key_cols)] * 3
    rows_wide = row_spec(value_cols)
    gain_spec = pl.BlockSpec((1, DV), lambda i: (0, 0))
    whole_state = pl.BlockSpec((H, DV, DK), lambda i: (i, 0, 0))
    wide_shape = jax.ShapeDtypeStruct((row_count, value_cols), bf16)
    block_flops = 2 * SPAN * DK * DV * 6

    def to_heads(array):
        rows = array.shape[2]
        return lax.all_to_all(
            array.reshape(links.seq_count, rows, DK), "seq", split_axis=0, concat_axis=0, tiled=True
        )

    def to_tokens(array):
        back = lax.all_to_all(array, "seq", split_axis=0, concat_axis=0, tiled=True)
        return back.reshape(seq_count * H, DV, DK)

    inside, update = block_call(
        local_kernel,
        seq_count,
        qkg_specs + [rows_wide],
        [rows_wide, state_spec(groups, state_rows + 16)],
        [
            jax.ShapeDtypeStruct((row_count, value_cols), f32),
            jax.ShapeDtypeStruct((seq_count * H, groups, state_rows + 16, DK), bf16),
        ],
        2 * block_flops,
    )(query, keys, decay, values)
    y_gate = links.swap(fence(piece_gate, y_out, update)[0], "fsdp")
    near_up = links.swap(fence(piece_up, y_gate)[0], "fsdp")
    y_out = fence(y_out, update)[0]
    x_out = links.swap_by_core(y_out, near_bits)
    x_gate = links.swap_by_core(y_gate, near_bits)
    received = to_heads(update)
    before = scan_blocks(False, received, received)
    near_up, x_gate = fence(near_up, before)[0], fence(x_gate, before)[0]
    full_feed_down = lay_down(links, fence(feed_down, update)[0])
    full_output = lay_down(links, fence(output_weight, update)[0])
    near_down = near_half(links, y_out[: out_rows[0]], x_out[: out_rows[0]])
    near_output = near_half(links, y_out[out_rows[0] :], x_out[out_rows[0] :])
    far_out = links.swap(jnp.concatenate((near_down, near_output), axis=0), 0)
    far_down, far_output = far_out[: 2 * out_rows[0]], far_out[2 * out_rows[0] :]
    full_feed_down = fill_other(links, full_feed_down, near_down, far_down)
    full_output = fill_other(links, full_output, near_output, far_output)
    near_gate = near_half(links, y_gate, x_gate)
    far_gate = links.swap(near_gate, 0)
    far_up = links.swap(near_up, 0)
    d_down = cotangent.reshape(row_count, width)
    seq_grad = d_down.astype(f32)
    down_ours, down_theirs = half_columns(links, d_down, (width,))
    normed_both, down_both = with_other_core(
        links, (normed, down_ours), (fence(normed, update)[0], down_theirs)
    )
    state = to_tokens(before)
    mixed, gated = block_call(
        outside_kernel,
        seq_count,
        qkg_specs + [rows_wide, whole_state, rows_wide, gain_spec],
        [rows_wide] * 2,
        [wide_shape] * 2,
        block_flops,
    )(query, keys, decay, inside, state, out_gate, head_gain_row)


    gated = fence(gated, normed_both, down_both)[0]
    middle = residual_in + mat_product(gated, full_output)
    second_full, second_pull = jax.vjp(rms_scale, middle, full_feed_gain.astype(f32))
    second_norm = second_full.astype(bf16)
    half = width // 2
    other_base = (1 - links.fsdp) * half
    places = jnp.stack(
        (links.fsdp * half, other_base + core * (half // 2), other_base + (1 - core) * (half // 2))
    ).astype(jnp.int32)
    hidden, d_gate, d_up, fed, d_second = feed_forward(
        places,
        second_norm,
        d_down,
        (feed_gate, near_gate, far_gate),
        (feed_up, near_up, far_up),
        full_feed_down,
    )
    output = (middle + fed).astype(bf16).reshape(seq_count, seg_rows, width)

    (second_both,) = with_other_core(links, (second_norm,), (second_norm,))
    (hidden_both,) = with_other_core(links, (hidden,), (hidden,))
    grad_down = cross_rows(hidden_both, down_both).astype(bf16)

    x, y, z = 1, "fsdp", 2
    cuts = (([y, x, z], [x, z, y]), ([y, z, x], [z, x, y]), ([y, x, z], [y, z, x]))
    joins = ([z, x], [x, z])
    shares, arrived, sent, extras = {}, [], [], []

    def after_last(array):
        return fence(array, *sent[-1:])[0]

    def hold(array, *due):
        behind = (*arrived[-4:-3], *sent[-1:], *extras, *due)
        sent.append(array)
        return fence(array, *behind)[0]

    def go(*names):
        for name in names:
            share = shares[name]
            if not share.steps:
                share.receive(after_last)
                sent.append(share.outs[0])
                continue
            arrived.append(share.step(after_last, hold))
            while share.steps and share.steps[0][0] == "meet" and share.steps[0][1][0] > 3:
                arrived.append(share.step(after_last, hold))

    shares["down"] = Share(links, grad_down[None], [(width,)], cuts[0], joins)
    go("down")
    d_second = fence(d_second, sent[0])[0]

    gate_ours, gate_theirs = half_columns(links, d_gate, (hidden_width,))
    up_ours, up_theirs = half_columns(links, d_up, (hidden_width,))
    gate_both, up_both = with_other_core(links, (gate_ours, up_ours), (gate_theirs, up_theirs))
    grad_gate = cross_rows(second_both, gate_both).astype(bf16)
    grad_up = cross_rows(second_both, up_both).astype(bf16)

    d_middle_norm, grad_feed_gain = second_pull(d_second)
    d_middle = seq_grad + d_middle_norm
    d_branch = d_middle.astype(bf16)
    d_gated = back_product(d_branch, full_output)
    d_mixed, d_outgate, gain_parts, back_update = block_call(
        back_state_kernel,
        seq_count,
        qkg_specs + [rows_wide] * 3 + [gain_spec],
        [rows_wide] * 2
        + [pl.BlockSpec((1, 8, DV), lambda i: (i, 0, 0)), state_spec(groups, state_rows)],
        [wide_shape] * 2
        + [
            jax.ShapeDtypeStruct((seq_count, 8, DV), f32),
            jax.ShapeDtypeStruct((seq_count * H, groups, state_rows, DK), bf16),
        ],
        block_flops,
    )(query, keys, decay, d_gated, mixed, out_gate, head_gain_row)
    grad_head_gain = jnp.sum(gain_parts, axis=(0, 1))
    branch_ours, branch_theirs = half_columns(links, d_branch, (width,))
    outgate_ours, outgate_theirs = half_columns(links, d_outgate, (value_cols,))
    gated_both, branch_both, outgate_both = with_other_core(
        links, (gated, branch_ours, outgate_ours), (gated, branch_theirs, outgate_theirs)
    )
    grad_mixer_out = fence(
        jnp.stack(
            (
                cross_rows(gated_both, branch_both).astype(bf16),
                cross_rows(normed_both, outgate_both).astype(bf16),
            )
        )
    )[0]

    back_received = to_heads(hold(back_update))
    shares["gate"] = Share(links, grad_gate[None], [(hidden_width,)], cuts[1], joins)
    shares["out"] = Share(links, grad_mixer_out, [(width,), (value_cols,)], cuts[0], joins)
    shares["up"] = Share(links, grad_up[None], [(hidden_width,)], cuts[2], joins)
    go("gate", "out", "down")
    after = to_tokens(hold(scan_blocks(True, received, after_last(back_received))))
    go("up", "gate", "down")
    after = after_last(after)
    d_query, d_keys, d_decay, d_values = block_call(
        back_kernel,
        seq_count,
        qkg_specs + [rows_wide] * 2 + [whole_state] * 2,
        [row_spec(key_cols)] * 3 + [rows_wide],
        [jax.ShapeDtypeStruct((row_count, key_cols), bf16)] * 3 + [wide_shape],
        4 * block_flops,
    )(query, keys, decay, values, d_mixed, state, after)
    d_qkv = jnp.concatenate((d_query, d_keys, d_values), axis=1)
    qkv_ours, qkv_theirs = half_columns(links, d_qkv, in_widths[:3])
    (qkv_both,) = with_other_core(links, (qkv_ours,), (qkv_theirs,))
    grad_qkv = cross_rows(normed_both, qkv_both).astype(bf16)
    shares["qkv"] = Share(links, grad_qkv[None], [in_widths[:3]], cuts[1], joins)
    sent.append(d_query)
    go("qkv")
    d_qkv, d_decay, _ = fence(d_qkv, d_decay, sent[-1])

    d_decay_in = d_decay.astype(f32) * jax.nn.sigmoid(-decay_in) / gate_scale
    grad_decay_bias = jnp.sum(d_decay_in, axis=0)
    grad_decay_up = lax.dot_general(
        ranked.astype(f32), d_decay_in, (((0,), (0,)), ((), ())), precision=highest
    )
    d_ranked = lax.dot_general(
        d_decay_in, full_up_rank.astype(f32), (((1,), (1,)), ((), ())), precision=highest
    ).astype(bf16)
    grad_decay_down = cross_rows(normed, d_ranked)
    d_normed = back_product(
        jnp.concatenate((d_qkv, d_outgate), axis=1), full_in
    ) + back_product(d_ranked, full_down)
    d_input_norm, grad_mixer_gain = first_pull(d_normed)
    input_grad = (d_middle + d_input_norm).reshape(seq_count, seg_rows, width)

    small_grads = (
        grad_mixer_gain, grad_decay_down, grad_decay_up, grad_decay_bias, grad_head_gain,
        grad_feed_gain,
    )
    total = jnp.concatenate([grad.reshape(2, -1) for grad in small_grads], axis=1)
    go("up", "gate", "down", "out")
    other = links.swap(hold(pick(total, 1 - links.fsdp), input_grad, output), "fsdp")
    go("up", "qkv", "gate")
    total = (pick(total, links.fsdp) + after_last(other)).reshape(links.seq_count, -1)
    pieces = lax.all_to_all(hold(total), "seq", split_axis=0, concat_axis=0, tiled=True)
    go("out", "qkv", "up", "gate")
    own_sum = jnp.sum(after_last(pieces), axis=0, keepdims=True)
    own_sum = hold(jnp.broadcast_to(own_sum, total.shape))
    total = lax.all_to_all(own_sum, "seq", split_axis=0, concat_axis=0, tiled=True)
    go("down", "out", "up", "down", "qkv", "gate")
    total = after_last(total).reshape(-1)
    small_out = []
    offset = 0
    for grad in small_grads:
        size = grad.size // 2
        small_out.append(
            total[offset : offset + size].reshape((grad.shape[0] // 2,) + grad.shape[1:])
        )
        offset += size
    out_mixer_gain, out_decay_down, out_decay_up, out_bias, out_head_gain, out_feed_gain = small_out
    extras.extend(small_out)
    go("qkv", "out", "up", "down", "qkv", "down", "out", "gate", "qkv", "up", "gate", "out", "qkv", "up", "out")
    results = [
        out for name in ("down", "gate", "up", "out", "qkv") for out in shares[name].outs
    ]


    (
        out_down, out_gate_w, out_up_w, out_output, out_outgate, out_query, out_key, out_value,
    ) = results
    return (
        output,
        input_grad,
        out_mixer_gain,
        out_query,
        out_key,
        out_value,
        out_decay_down,
        out_decay_up,
        out_bias,
        out_outgate,
        out_head_gain,
        out_output,
        out_feed_gain,
        out_gate_w,
        out_up_w,
        out_down,
    )


def solution(mesh):
    rows = P("fsdp", None)
    gains = P("fsdp")
    tokens = P("fsdp", "seq", None)
    weights = (gains, rows, rows, rows, rows, rows, gains, rows, gains, rows, gains, rows, rows, rows)
    return jax.shard_map(
        per_device,
        mesh=mesh,
        in_specs=(tokens,) + weights + (tokens,),
        out_specs=(tokens, tokens) + weights,
        check_vma=False,
    )
```
